512 devices in a mesh: lat: 2 (over core), lon: 32 (over z_hi, y, x), tp: 8 (over z_lo).
Axes of the slice: x: 4, y: 4, z: 16 (z_hi: 2, z_lo: 8; z = z_hi * 8 + z_lo), core: 2. Of those that a mesh axis runs over, the one named last changes fastest.
Arguments:
- fine_tokens: bfloat16 [2, 24, 1536, 512], P(None, 'lat', ('lon', 'tp')), may hold values from -6 to 6
- fine_qkv: bfloat16 [512, 1536], replicated, may hold values from -1.5 to 1.5
- fine_out: bfloat16 [512, 512], replicated, may hold values from -0.25 to 0.25
- merge_weight: bfloat16 [2048, 1024], P(None, 'tp'), may hold values from -0.125 to 0.125
- up_weight: bfloat16 [1024, 4096], P(None, 'tp'), may hold values from -0.1875 to 0.1875
- down_weight: bfloat16 [4096, 1024], P('tp'), may hold values from -0.09375 to 0.09375
- cotangent: bfloat16 [2, 12, 768, 1024], P(None, 'lat', ('lon', 'tp')), may hold values from -24 to 24
Outputs:
- coarse_out: bfloat16 [2, 12, 768, 1024], P(None, 'lat', ('lon', 'tp'))
- grad_merged: bfloat16 [2, 12, 768, 1024], P(None, 'lat', ('lon', 'tp'))
- grad_down: float32 [4096, 1024], P('tp', ('lat', 'lon'))
The draws below stay inside these ranges and needn't reach their ends.
All inputs are finite; a program needn't handle non-finite values.
Results may differ from the reference program's by a relative error of at most 0.023.
The reference program's roundings to bfloat16 on the way count: a program that leaves them out, or rounds other values in their place, can miss the bound.
Values may be sent and summed in bfloat16 or wider, within the bound.
No kernel may reach another device: no remote copies, remote signals or barrier semaphores. Data moves between devices by JAX's collectives and lax.ppermute only.
A program may use at most 64 MiB of HBM per device.

```python
import math
import jax
import jax.numpy as jnp
from jax import lax

C = 512
HEAD_DIM = 32
FF = 4096
LEV = 2
CC = 1024
NLAT = 24
NLON = 1536
N_TP = 8


def draw_fine_qkv(key, part):
    key = jax.random.fold_in(key, 7)
    weights = jax.random.normal(key, (C, 3 * C), jnp.float32) / math.sqrt(C)
    return jnp.clip(weights, -1.5, 1.5).astype(jnp.bfloat16)


def with_spikes(array, key, source, target, shards_of, factor):
    owner, partner = [(jnp.arange(array.shape[position]) // (array.shape[position] // shards_of)).reshape([-1 if axis == position else 1 for axis in range(array.ndim)]) for position in (source, target)]
    chosen = jax.random.permutation(key, shards_of)[partner]
    strong = (owner == chosen) | (owner == (partner + shards_of // 2) % shards_of)
    return jnp.where(strong, factor * array, array)


def shard_levels(key, shape, cuts, smallest, largest):
    def one(position, blocks):
        steps = jax.random.uniform(jax.random.fold_in(jax.random.fold_in(key, 6), position), (blocks,), jnp.float32, smallest / len(cuts), largest / len(cuts))
        return jnp.repeat(jnp.exp(steps), shape[position] // blocks).reshape((-1,) + (1,) * (len(shape) - position - 1))

    gain = one(*cuts[0])
    for cut in cuts[1:]:
        gain = gain * one(*cut)
    return gain


def scatter_about(key, dims, width, limit, pieces=(), kind=jnp.bfloat16):
    factor_of = shard_levels(key, dims, pieces, -0.22, 0.18) if pieces else 1.0
    result = jax.random.normal(key, dims, jnp.float32) * width * factor_of
    return jnp.minimum(jnp.maximum(result, -limit), limit).astype(kind)


def noise_with(key, extent, scale, most, split, heavy, dtype=jnp.bfloat16):
    entries = scale * jax.random.normal(key, extent, jnp.float32)
    if split:
        entries = entries * shard_levels(key, extent, split, -0.22, 0.18)
    return jnp.clip(with_spikes(entries, jax.random.fold_in(key, 3), *heavy), -most, most).astype(dtype)


def setup_inputs(seed: int = 0) -> dict:
    keys = jax.random.split(jax.random.key(seed), 8)
    return {
        "fine_tokens": scatter_about(keys[0], (LEV, NLAT, NLON, C), 1.0, 6.0, ((1, 2), (2, 256))),
        "fine_qkv": draw_fine_qkv(jax.random.fold_in(keys[7], 71), 0),
        "fine_out": scatter_about(keys[2], (C, C), C ** -0.5, 0.25),
        "merge_weight": scatter_about(keys[3], (4 * C, CC), (4 * C) ** -0.5, 0.125, ((1, 8),)),
        "up_weight": scatter_about(keys[4], (CC, FF), CC ** -0.5, 0.1875, ((1, 8),)),
        "down_weight": scatter_about(keys[5], (FF, CC), FF ** -0.5, 0.09375, ((0, 8),)),
        "cotangent": noise_with(keys[6], (LEV, NLAT // 2, NLON // 2, CC), 1.0, 24.0, ((1, 2), (2, 256)), (2, 3, 256, 6.0)),
    }


EPS = 1e-05

def norm_rows(values):
    values = values.astype(jnp.float32)
    centred = values - lax.optimization_barrier(jnp.mean(values, axis=-1, keepdims=True))
    variance = lax.optimization_barrier(jnp.mean(centred * centred, axis=-1, keepdims=True))
    return centred * lax.rsqrt(variance + EPS)

def gelu_exact(values):
    return jax.nn.gelu(values, approximate=False)

def to_windows(block):
    levels, lat_rows, columns, feats = block.shape
    shaped = block.reshape(levels // 2, 2, lat_rows // 12, 12, columns // 6, 6, feats)
    return shaped.transpose(4, 0, 2, 1, 3, 5, 6).reshape(-1, 144, feats)

def from_windows(windows, levels, lat_rows, columns):
    feats = windows.shape[-1]
    shaped = windows.reshape(columns // 6, levels // 2, lat_rows // 12, 2, 12, 6, feats)
    return shaped.transpose(1, 3, 2, 4, 0, 5, 6).reshape(levels, lat_rows, columns, feats)

def attend_window(window):
    heads = C // HEAD_DIM
    queries = window[:, :C].astype(jnp.float32).reshape(144, heads, HEAD_DIM)
    key_rows = window[:, C:2 * C].astype(jnp.float32).reshape(144, heads, HEAD_DIM)
    value_rows = window[:, 2 * C:].astype(jnp.float32).reshape(144, heads, HEAD_DIM)
    scores = jnp.einsum('qhd,khd->hqk', queries, key_rows) * HEAD_DIM ** (-0.5)
    probs = jax.nn.softmax(scores, axis=-1).astype(jnp.bfloat16)
    mixed = jnp.einsum('hqk,khd->qhd', probs.astype(jnp.float32), value_rows)
    return mixed.astype(jnp.bfloat16).reshape(144, C)

def reference(fine_tokens, fine_qkv, fine_out, merge_weight, up_weight, down_weight, cotangent):
    normed = norm_rows(fine_tokens).astype(jnp.bfloat16)
    packed = jnp.dot(normed.reshape(-1, C), fine_qkv, preferred_element_type=jnp.float32)
    packed = packed.astype(jnp.bfloat16).reshape(LEV, NLAT, NLON, 3 * C)
    rolled = jnp.roll(packed, -3, axis=2)
    windows = to_windows(rolled).reshape(NLON // 6, -1, 144, 3 * C)
    mixed = lax.map(lambda group: jax.vmap(attend_window)(group), windows)
    mixed = from_windows(mixed.reshape(-1, 144, C), LEV, NLAT, NLON)
    mixed = jnp.roll(mixed, 3, axis=2)
    projected = jnp.dot(mixed.reshape(-1, C), fine_out, preferred_element_type=jnp.float32)
    section = (fine_tokens.astype(jnp.float32) + projected.reshape(LEV, NLAT, NLON, C)).astype(jnp.bfloat16)
    blocks = section.reshape(LEV, NLAT // 2, 2, NLON // 2, 2, C).transpose(0, 1, 3, 2, 4, 5)
    merged_in = norm_rows(blocks.reshape(-1, 4 * C)).astype(jnp.bfloat16)
    merged = jnp.dot(merged_in, merge_weight, preferred_element_type=jnp.float32).astype(jnp.bfloat16)
    coarse_normed = norm_rows(merged).astype(jnp.bfloat16)
    preact = jnp.dot(coarse_normed, up_weight, preferred_element_type=jnp.float32)
    hidden_f, gelu_back = jax.vjp(gelu_exact, preact)
    hidden = hidden_f.astype(jnp.bfloat16)
    block_units = FF // N_TP
    summed = jnp.zeros(merged.shape, jnp.float32)
    grad_normed = jnp.zeros(merged.shape, jnp.float32)
    flat_cot = cotangent.reshape(-1, CC)
    grad_hidden = lax.dot_general(flat_cot, down_weight, (((1,), (1,)), ((), ())), preferred_element_type=jnp.float32)
    grad_preact = gelu_back(grad_hidden)[0].astype(jnp.bfloat16)
    for index in range(N_TP):
        lower = index * block_units
        partial_value = jnp.dot(hidden[:, lower:lower + block_units], down_weight[lower:lower + block_units], preferred_element_type=jnp.float32)
        partial_value = lax.optimization_barrier(partial_value.astype(jnp.bfloat16))
        summed = summed + partial_value.astype(jnp.float32)
        back_part = lax.dot_general(grad_preact[:, lower:lower + block_units], up_weight[:, lower:lower + block_units], (((1,), (1,)), ((), ())), preferred_element_type=jnp.float32)
        back_part = lax.optimization_barrier(back_part.astype(jnp.bfloat16))
        grad_normed = grad_normed + back_part.astype(jnp.float32)
    coarse_out = (merged.astype(jnp.float32) + summed).astype(jnp.bfloat16)
    merged_f = merged.astype(jnp.float32)
    centred = merged_f - lax.optimization_barrier(jnp.mean(merged_f, axis=-1, keepdims=True))
    scale_inv = lax.rsqrt(lax.optimization_barrier(jnp.mean(centred * centred, axis=-1, keepdims=True)) + EPS)
    nhat = centred * scale_inv
    grad_merged = flat_cot.astype(jnp.float32) + scale_inv * (grad_normed - lax.optimization_barrier(jnp.mean(grad_normed, axis=-1, keepdims=True)) - nhat * lax.optimization_barrier(jnp.mean(grad_normed * nhat, axis=-1, keepdims=True)))
    grad_down = lax.dot_general(hidden, flat_cot, (((0,), (0,)), ((), ())), preferred_element_type=jnp.float32)
    out_shape = (LEV, NLAT // 2, NLON // 2, CC)
    return (coarse_out.reshape(out_shape), grad_merged.astype(jnp.bfloat16).reshape(out_shape), grad_down)
```

```python
import functools

import jax
import jax.numpy as jnp
import numpy as np
from jax import lax
from jax.experimental import pallas as pl
from jax.experimental.pallas import tpu as pltpu
from jax.sharding import PartitionSpec as P

EPS = 1e-05
F32 = jnp.float32
BF16 = jnp.bfloat16
LINE = ("lon", "tp")
COUNT = 256
RING = (0, 1, 3, 2)
ROWS = 40


def dot(a, b):
    return lax.dot_general(a, b, (((1,), (0,)), ((), ())), preferred_element_type=F32)


def dot_nt(a, b):
    return lax.dot_general(a, b, (((1,), (1,)), ((), ())), preferred_element_type=F32)


def dot_tn(a, b):
    return lax.dot_general(a, b, (((0,), (0,)), ((), ())), preferred_element_type=F32)


def moved(value, target):
    return lax.ppermute(value, LINE, [(s, target(s)) for s in range(COUNT)])


def swapped(value, bits):
    return moved(value, lambda s: s ^ bits)


def across(value):
    return lax.ppermute(value, "lat", [(0, 1), (1, 0)])


def z_bits(index):
    return index


def x_bits(index):
    return index << 3


def y_bits(index):
    return index << 5


Z_HALF = 4
Z_HI = 1 << 7


def norm_rows(values):
    centred = values - jnp.mean(values, axis=-1, keepdims=True)
    variance = jnp.mean(centred * centred, axis=-1, keepdims=True)
    return centred * lax.rsqrt(variance + EPS)


def call(kernel, out_shape, *args, flops=0, scalars=0, **kw):
    specs = [
        pl.BlockSpec(memory_space=pltpu.SMEM if i < scalars else pltpu.VMEM)
        for i in range(len(args))
    ]
    size = sum(a.size * a.dtype.itemsize for a in args)
    return pl.pallas_call(
        kernel,
        out_shape=out_shape,
        in_specs=specs,
        out_specs=jax.tree.map(lambda _: pl.BlockSpec(memory_space=pltpu.VMEM), out_shape),
        compiler_params=pltpu.CompilerParams(vmem_limit_bytes=40 * 1024 * 1024),
        cost_estimate=pl.CostEstimate(flops=flops, bytes_accessed=size, transcendentals=0),
        **kw,
    )(*args)


def shaped(shape, dtype=BF16):
    return jax.ShapeDtypeStruct(shape, dtype)


def merge_order():
    order = np.zeros((4 * ROWS, 144), np.float32)
    for quarter in range(4):
        d_lat, d_lon = quarter // 2, quarter % 2
        for token in range(36):
            lat, lon, lev = token // 6, token % 6 // 2, token % 2
            row, column = 2 * lat + d_lat, 2 * lon + d_lon
            source = 72 * (column // 3) + 6 * row + 2 * (column % 3) + lev
            order[ROWS * quarter + token, source] = 1.0
    return order.astype(jnp.bfloat16)


def attend_kernel(own0, own1, west, east, qkv, out_w, order, result):
    tokens = jnp.concatenate(
        [r[...].astype(F32) for r in (own0, own1, west, east)], axis=0
    )
    normed = norm_rows(tokens).astype(BF16)
    packed = dot(normed, qkv[...]).astype(BF16).astype(F32)
    lane = lax.broadcasted_iota(jnp.int32, (1, 128), 1) // 32
    masks = [(lane == h).astype(F32) for h in range(4)]
    scale = 32 ** -0.5
    halves = []
    for window in range(2):
        rows = slice(72 * window, 72 * window + 72)
        other = slice(144 + 72 * window, 216 + 72 * window)
        parts = []
        for group in range(4):
            low = 128 * group
            queries = packed[rows, low : low + 128]
            keys = jnp.concatenate(
                [packed[rows, 512 + low : 640 + low], packed[other, 512 + low : 640 + low]], axis=0
            ).astype(BF16)
            values = jnp.concatenate(
                [packed[rows, 1024 + low : 1152 + low], packed[other, 1024 + low : 1152 + low]], axis=0
            ).astype(BF16)
            stacked = jnp.concatenate([queries * m for m in masks], axis=0).astype(BF16)
            scores = dot_nt(stacked, keys) * scale
            scores = scores - jnp.max(scores, axis=-1, keepdims=True)
            scores = jnp.exp(scores)
            probs = (scores / jnp.sum(scores, axis=-1, keepdims=True)).astype(BF16)
            mixed = dot(probs, values)
            total = mixed[0:72] * masks[0]
            for h in range(1, 4):
                total = total + mixed[72 * h : 72 * h + 72] * masks[h]
            parts.append(total)
        halves.append(jnp.concatenate(parts, axis=1))
    mixed = jnp.concatenate(halves, axis=0).astype(BF16)
    section = (tokens[0:144] + dot(mixed, out_w[...])).astype(BF16)
    spread = dot(order[...], section)
    wide = jnp.concatenate([spread[ROWS * q : ROWS * q + ROWS] for q in range(4)], axis=1)
    result[...] = norm_rows(wide).astype(BF16)


def merge_kernel(b0, b1, b2, b3, own_w, far_w, result):
    blocks = jnp.concatenate([b[...].astype(F32) for b in (b0, b1, b2, b3)], axis=0).astype(BF16)
    for half, weight in enumerate((own_w, far_w)):
        part = dot(blocks, weight[...])
        for j in range(4):
            result[j, :, 128 * half : 128 * half + 128] = part[ROWS * j : ROWS * j + ROWS].astype(BF16)


def pack_kernel(place, merge, up, down, packed):
    r = place[0]
    packed[0:32, :] = up[pl.ds(pl.multiple_of(r * 32, 32), 32), :]
    half = lax.rem(r, 2)
    row = pl.multiple_of((r // 2) * 32, 32)
    packed[32:64, :] = down[pl.ds(row, 32), pl.ds(pl.multiple_of(half * 512, 512), 512)]
    for q in range(4):
        packed[64:80, 128 * q : 128 * q + 128] = merge[pl.ds(pl.multiple_of(512 * q + r * 16, 16), 16), :]


def unpack_kernel(place, near, far, merge, up, down):
    for side, source in enumerate((near, far)):
        for b in range(4):
            for a in range(4):
                r = (place[0] ^ side) * 16 + (place[1] ^ RING[b]) * 4 + (place[2] ^ RING[a])
                piece = 4 * b + a
                up[pl.ds(pl.multiple_of(r * 32, 32), 32), :] = source[piece, 0:32, :]
                row = pl.multiple_of((r // 2) * 32, 32)
                column = pl.multiple_of(lax.rem(r, 2) * 512, 512)
                down[pl.ds(row, 32), pl.ds(column, 512)] = source[piece, 32:64, :]
                for q in range(4):
                    at = pl.multiple_of(512 * q + r * 16, 16)
                    merge[pl.ds(at, 16), :] = source[piece, 64:80, 128 * q : 128 * q + 128]


def far_weights(place, merge, up, down):
    lat, y, x = place[0], place[1], place[2]
    index = (lat * 16 + y * 4 + x).reshape(1)
    packed = call(pack_kernel, shaped((80, 512)), index, merge, up, down, scalars=1)
    held = swapped(packed, Z_HALF)[None]
    for axis_bits in (x_bits, y_bits):
        for step in (1, 3):
            held = jnp.concatenate([held, swapped(held, axis_bits(step))], axis=0)
    other = across(held)
    return call(
        unpack_kernel,
        (shaped((2048, 128)), shaped((1024, 512)), shaped((512, 1024))),
        place,
        held,
        other,
        scalars=1,
    )


def gelu_parts(values):
    cdf = 0.5 * (1.0 + lax.erf(values * np.float32(np.sqrt(0.5))))
    density = jnp.exp(-0.5 * values * values) * np.float32(1.0 / np.sqrt(2.0 * np.pi))
    return values * cdf, cdf + values * density


def feed_kernel(
    place, m0, m1, m2, m3, c0, c1, c2, c3, up0, up1, down0, down1,
    own_merged, s0, s1, s2, s3, hidden_out, merged, hidden, grad,
):
    th, tl = place[3], place[4]
    for j, source in enumerate((m0, m1, m2, m3)):
        for half in range(2):
            column = ((th ^ half) * 4 + (tl ^ j)) * 128
            column = pl.multiple_of(column, 128)
            for block in range(4):
                merged[ROWS * block : ROWS * block + ROWS, pl.ds(column, 128)] = source[
                    block ^ j, :, 128 * half : 128 * half + 128
                ].astype(F32)
    own_merged[...] = merged[0:ROWS, :].astype(BF16)
    normed = norm_rows(merged[...]).astype(BF16)
    cots = jnp.concatenate([c[...].astype(F32) for c in (c0, c1, c2, c3)], axis=0).astype(BF16)
    for half, (up, down) in enumerate(((up0, down0), (up1, down1))):
        columns = slice(512 * half, 512 * half + 512)
        value, slope = gelu_parts(dot(normed, up[...]))
        hidden[:, columns] = value.astype(BF16)
        grad[:, columns] = (dot_nt(cots, down[...]) * slope).astype(BF16)
    hidden_out[...] = hidden[...]
    partial = dot(hidden[:, 0:512], down0[...]) + dot(hidden[:, 512:1024], down1[...])
    back = dot_nt(grad[:, 0:512], up0[...]) + dot_nt(grad[:, 512:1024], up1[...])
    for j, sent in enumerate((s0, s1, s2, s3)):
        rows = slice(ROWS * j, ROWS * j + ROWS)
        sent[0] = partial[rows].astype(BF16)
        sent[1] = back[rows].astype(BF16)


def finish_kernel(merged, cot, s0, r1, r2, r3, coarse_out, grad_merged):
    merged_f = merged[...].astype(F32)
    summed = s0[0].astype(F32) + r1[0].astype(F32) + r2[0].astype(F32) + r3[0].astype(F32)
    coarse_out[...] = (merged_f + summed).astype(BF16)
    grad_normed = s0[1].astype(F32) + r1[1].astype(F32) + r2[1].astype(F32) + r3[1].astype(F32)
    centred = merged_f - jnp.mean(merged_f, axis=-1, keepdims=True)
    scale_inv = lax.rsqrt(jnp.mean(centred * centred, axis=-1, keepdims=True) + EPS)
    nhat = centred * scale_inv
    grad = cot[...].astype(F32) + scale_inv * (
        grad_normed
        - jnp.mean(grad_normed, axis=-1, keepdims=True)
        - nhat * jnp.mean(grad_normed * nhat, axis=-1, keepdims=True)
    )
    grad_merged[...] = grad.astype(BF16)


def column_kernel(place, c0, c1, c2, c3, near, far):
    cots = jnp.concatenate([c[...].astype(F32) for c in (c0, c1, c2, c3)], axis=0).astype(BF16)
    lat, y, x, zh = place[0], place[1], place[2], place[5]
    source = lax.broadcasted_iota(jnp.int32, (512, 512), 0)
    target = lax.broadcasted_iota(jnp.int32, (512, 512), 1)
    x_part, y_part, z_part = target >> 7, (target >> 5) & 3, (target >> 4) & 1
    x_abs = (x_part ^ (x_part >> 1)) ^ x
    y_abs = (y_part ^ (y_part >> 1)) ^ y
    wanted = (((z_part ^ zh) * 4 + y_abs) * 4 + x_abs) * 16 + (target & 15)
    chosen = jnp.where(source == wanted, 1.0, 0.0).astype(BF16)
    low, high = cots[:, 0:512], cots[:, 512:1024]
    mine = jnp.where(lat == 0, low.astype(F32), high.astype(F32)).astype(BF16)
    theirs = jnp.where(lat == 0, high.astype(F32), low.astype(F32)).astype(BF16)
    near[...] = dot(mine, chosen).astype(BF16)
    far[...] = dot(theirs, chosen).astype(BF16)


def weight_kernel(near, near_hidden, far, far_hidden, kept, sent):
    rows = jnp.concatenate([near[...].astype(F32), far[...].astype(F32)], axis=0).astype(BF16)
    hidden = jnp.concatenate([near_hidden[...].astype(F32), far_hidden[...].astype(F32)], axis=0).astype(BF16)
    total = dot_tn(rows, hidden)
    kept[...] = total[0:256]
    sent[...] = total[256:512].astype(BF16)


def add_kernel(kept, got, left, sent):
    half = left.shape[0]
    total = kept[...] + got[...].astype(F32)
    left[...] = total[0:half]
    sent[...] = total[half:].astype(BF16)


def last_kernel(kept, got, left, sent):
    total = kept[...] + got[...].astype(F32)
    left[...] = total[:, 0:512]
    sent[...] = total[:, 512:1024].astype(BF16)


def token_rows(block):
    return block.transpose(1, 2, 0, 3).reshape(-1, block.shape[-1])


def on_device(fine_tokens, fine_qkv, fine_out, merge_weight, up_weight, down_weight, cotangent):
    lon, tp = lax.axis_index("lon"), lax.axis_index("tp")
    place = jnp.stack(
        [lax.axis_index("lat"), (lon >> 2) & 3, lon & 3, tp >> 2, tp & 3, lon >> 4]
    ).astype(jnp.int32)

    own0 = token_rows(fine_tokens[:, :, :3])
    own1 = token_rows(fine_tokens[:, :, 3:])
    west = moved(own1, lambda s: (s + 1) % COUNT)
    east = moved(own0, lambda s: (s - 1) % COUNT)

    far_merge, far_up, far_down = far_weights(place, merge_weight, up_weight, down_weight)

    cot = jnp.pad(token_rows(cotangent), ((0, ROWS - 36), (0, 0)))
    cots = [cot] + [swapped(cot, z_bits(j)) for j in (1, 2, 3)]

    merged_in = call(
        attend_kernel, shaped((ROWS, 2048)), own0, own1, west, east, fine_qkv, fine_out,
        jnp.asarray(merge_order()), flops=10**9,
    )
    ins = [merged_in] + [swapped(merged_in, z_bits(j)) for j in (1, 2, 3)]
    columns = call(merge_kernel, shaped((4, ROWS, 256)), *ins, merge_weight, far_merge, flops=2 * 10**8)
    held = [columns] + [swapped(columns, z_bits(j)) for j in (1, 2, 3)]

    near_cot, far_cot = call(
        column_kernel, (shaped((4 * ROWS, 512)), shaped((4 * ROWS, 512))), place, *cots, scalars=1, flops=10**8
    )
    other_cot = across(far_cot)

    own_merged, *sent, hidden = call(
        feed_kernel,
        (shaped((ROWS, 1024)),) + tuple(shaped((2, ROWS, 1024)) for _ in range(4)) + (shaped((4 * ROWS, 1024)),),
        place, *held, *cots, up_weight, far_up, down_weight, far_down,
        scalars=1, flops=2 * 10**9,
        scratch_shapes=[
            pltpu.VMEM((4 * ROWS, 1024), F32),
            pltpu.VMEM((4 * ROWS, 1024), BF16),
            pltpu.VMEM((4 * ROWS, 1024), BF16),
        ],
    )
    got = [swapped(sent[j], z_bits(j)) for j in (1, 2, 3)]
    other_hidden = across(hidden)

    kept, out = call(
        weight_kernel, (shaped((256, 1024), F32), shaped((256, 1024))),
        near_cot, hidden, other_cot, other_hidden, flops=3 * 10**8,
    )
    for bits, rows in ((x_bits(3), 128), (x_bits(1), 64), (y_bits(3), 32), (y_bits(1), 16)):
        kept, out = call(
            add_kernel, (shaped((rows, 1024), F32), shaped((rows, 1024))), kept, swapped(out, bits)
        )
    kept, out = call(
        last_kernel, (shaped((16, 512), F32), shaped((16, 512))), kept, swapped(out, Z_HI)
    )
    grad_down = (kept + swapped(out, Z_HALF).astype(F32)).T

    coarse_out, grad_merged = call(
        finish_kernel, (shaped((ROWS, 1024)), shaped((ROWS, 1024))), own_merged, cot, sent[0], *got
    )

    def placed(rows):
        return rows[:36].reshape(6, 3, 2, 1024).transpose(2, 0, 1, 3)

    return placed(coarse_out), placed(grad_merged), grad_down


def solution(mesh):
    tokens = P(None, "lat", ("lon", "tp"), None)
    return jax.shard_map(
        on_device,
        mesh=mesh,
        in_specs=(tokens, P(), P(), P(None, "tp"), P(None, "tp"), P("tp", None), tokens),
        out_specs=(tokens, tokens, P("tp", ("lat", "lon"))),
        check_vma=False,
    )
```

```python
import functools

import jax
import jax.numpy as jnp
import numpy as np
from jax import lax
from jax.experimental import pallas as pl
from jax.experimental.pallas import tpu as pltpu
from jax.sharding import PartitionSpec as P

EPS = 1e-05
F32 = jnp.float32
BF16 = jnp.bfloat16
LINE = ("lon", "tp")
COUNT = 256
RING = (0, 1, 3, 2)
ROWS = 40


def dot(a, b):
    return lax.dot_general(a, b, (((1,), (0,)), ((), ())), preferred_element_type=F32)


def dot_nt(a, b):
    return lax.dot_general(a, b, (((1,), (1,)), ((), ())), preferred_element_type=F32)


def dot_tn(a, b):
    return lax.dot_general(a, b, (((0,), (0,)), ((), ())), preferred_element_type=F32)


def moved(value, target):
    return lax.ppermute(value, LINE, [(s, target(s)) for s in range(COUNT)])


def swapped(value, bits):
    return moved(value, lambda s: s ^ bits)


def across(value):
    return lax.ppermute(value, "lat", [(0, 1), (1, 0)])


def x_bits(index):
    return index << 3


def y_bits(index):
    return index << 5


Z_HALF = 4
Z_HI = 1 << 7


def along_z(value):
    pairs = []
    for lat, steps in ((0, 4), (1, -4)):
        for lon in range(32):
            for tp in range(8):
                z = ((lon >> 4) * 8 + tp + steps) % 16
                target = (z >> 3) * 128 + (lon & 15) * 8 + (z & 7)
                pairs.append((lat * COUNT + lon * 8 + tp, lat * COUNT + target))
    return lax.ppermute(value, ("lat", "lon", "tp"), pairs)


def ring(value, low, steps):
    return moved(value, lambda s: (s & ~(3 << low)) | ((((s >> low) + steps) & 3) << low))


def norm_rows(values):
    centred = values - jnp.mean(values, axis=-1, keepdims=True)
    variance = jnp.mean(centred * centred, axis=-1, keepdims=True)
    return centred * lax.rsqrt(variance + EPS)


def call(kernel, out_shape, *args, flops=0, scalars=0, after=(), **kw):
    specs = [
        pl.BlockSpec(memory_space=pltpu.SMEM if i < scalars else pltpu.VMEM)
        for i in range(len(args))
    ] + [pl.BlockSpec(memory_space=pl.ANY) for _ in after]

    def body(*refs):
        kernel(*refs[: len(args)], *refs[len(args) + len(after) :])

    size = sum(a.size * a.dtype.itemsize for a in args)
    return pl.pallas_call(
        body,
        out_shape=out_shape,
        in_specs=specs,
        out_specs=jax.tree.map(lambda _: pl.BlockSpec(memory_space=pltpu.VMEM), out_shape),
        compiler_params=pltpu.CompilerParams(vmem_limit_bytes=40 * 1024 * 1024),
        cost_estimate=pl.CostEstimate(flops=flops, bytes_accessed=size, transcendentals=0),
        name=kernel.__name__,
        **kw,
    )(*args, *after)


def shaped(shape, dtype=BF16):
    return jax.ShapeDtypeStruct(shape, dtype)


def merge_order():
    order = np.zeros((4 * ROWS, 144), np.float32)
    for quarter in range(4):
        d_lat, d_lon = quarter // 2, quarter % 2
        for token in range(36):
            lat, lon, lev = token // 6, token % 6 // 2, token % 2
            row, column = 2 * lat + d_lat, 2 * lon + d_lon
            source = 72 * (column // 3) + 6 * row + 2 * (column % 3) + lev
            order[ROWS * quarter + token, source] = 1.0
    return order.astype(jnp.bfloat16)


def attend_kernel(own0, own1, west, east, qkv, out_w, order, cot, result):
    tokens = jnp.concatenate(
        [r[...].astype(F32) for r in (own0, own1, west, east)], axis=0
    )
    normed = norm_rows(tokens).astype(BF16)
    packed = dot(normed, qkv[...]).astype(BF16).astype(F32)
    lane = lax.broadcasted_iota(jnp.int32, (1, 128), 1) // 32
    masks = [(lane == h).astype(F32) for h in range(4)]
    scale = 32 ** -0.5
    halves = []
    for window in range(2):
        rows = slice(72 * window, 72 * window + 72)
        other = slice(144 + 72 * window, 216 + 72 * window)
        parts = []
        for group in range(4):
            low = 128 * group
            queries = packed[rows, low : low + 128]
            keys = jnp.concatenate(
                [packed[rows, 512 + low : 640 + low], packed[other, 512 + low : 640 + low]], axis=0
            ).astype(BF16)
            values = jnp.concatenate(
                [packed[rows, 1024 + low : 1152 + low], packed[other, 1024 + low : 1152 + low]], axis=0
            ).astype(BF16)
            stacked = jnp.concatenate([queries * m for m in masks], axis=0).astype(BF16)
            scores = dot_nt(stacked, keys) * scale
            scores = scores - jnp.max(scores, axis=-1, keepdims=True)
            scores = jnp.exp(scores)
            probs = (scores / jnp.sum(scores, axis=-1, keepdims=True)).astype(BF16)
            mixed = dot(probs, values)
            total = mixed[0:72] * masks[0]
            for h in range(1, 4):
                total = total + mixed[72 * h : 72 * h + 72] * masks[h]
            parts.append(total)
        halves.append(jnp.concatenate(parts, axis=1))
    mixed = jnp.concatenate(halves, axis=0).astype(BF16)
    section = (tokens[0:144] + dot(mixed, out_w[...])).astype(BF16)
    spread = dot(order[...], section)
    wide = jnp.concatenate([spread[ROWS * q : ROWS * q + ROWS] for q in range(4)], axis=1)
    result[:, 0:2048] = norm_rows(wide).astype(BF16)
    result[:, 2048:3072] = cot[...]


def stacked_rows(blocks, columns):
    return jnp.concatenate([b[:, columns].astype(F32) for b in blocks], axis=0).astype(BF16)


def merge_kernel(b0, b1, b2, b3, own_w, far_w, result):
    blocks = stacked_rows((b0, b1, b2, b3), slice(0, 2048))
    for half, weight in enumerate((own_w, far_w)):
        part = dot(blocks, weight[...])
        for j in range(4):
            result[j, :, 128 * half : 128 * half + 128] = part[ROWS * j : ROWS * j + ROWS].astype(BF16)


def pack_kernel(place, merge, up, down, packed):
    r = place[0] * 4 + (place[1] & 1) * 2 + (place[2] & 1)
    for half in range(2):
        packed[half, 0:64, :] = up[pl.ds(pl.multiple_of(r * 128 + 64 * half, 64), 64), :]
        packed[half, 64:128, :] = down[pl.ds(pl.multiple_of(r * 64, 64), 64), 512 * half : 512 * half + 512]
        for q in range(4):
            row = pl.multiple_of(512 * q + r * 64 + 32 * half, 32)
            packed[half, 128:160, 128 * q : 128 * q + 128] = merge[pl.ds(row, 32), :]


def split_kernel(both, first, second):
    first[...] = both[0]
    second[...] = both[1]


def pair_kernel(first, other_first, second, other_second, firsts, seconds):
    firsts[0], firsts[1] = first[...], other_first[...]
    seconds[0], seconds[1] = second[...], other_second[...]


def four_kernel(a, b, c, d, result):
    for index, part in enumerate((a, b, c, d)):
        result[2 * index], result[2 * index + 1] = part[0], part[1]


def unpack_kernel(place, a, b, c, d, far, merge, up, down):
    for side in range(2):
        for y in range(2):
            for half in range(2):
                source = (a, b, c, d)[2 * y + half]
                for x in range(2):
                    r = (place[0] ^ side) * 4 + ((place[1] & 1) ^ y) * 2 + ((place[2] & 1) ^ x)
                    piece = far.at[4 * y + 2 * half + x] if side else source.at[x]
                    up[pl.ds(pl.multiple_of(r * 128 + 64 * half, 64), 64), :] = piece[0:64, :]
                    row = pl.multiple_of(r * 64, 64)
                    down[pl.ds(row, 64), 512 * half : 512 * half + 512] = piece[64:128, :]
                    for q in range(4):
                        at = pl.multiple_of(512 * q + r * 64 + 32 * half, 32)
                        merge[pl.ds(at, 32), :] = piece[128:160, 128 * q : 128 * q + 128]


def gelu_parts(values):
    cdf = 0.5 * (1.0 + lax.erf(values * np.float32(np.sqrt(0.5))))
    density = jnp.exp(-0.5 * values * values) * np.float32(1.0 / np.sqrt(2.0 * np.pi))
    return values * cdf, cdf + values * density


def hidden_kernel(
    place, m0, m1, m2, m3, up0, up1, far_cot, own_merged, bundle, slope, merged
):
    th, tl = place[3], place[4]
    for j, source in enumerate((m0, m1, m2, m3)):
        for half in range(2):
            column = ((th ^ half) * 4 + (tl ^ j)) * 128
            column = pl.multiple_of(column, 128)
            for block in range(4):
                merged[ROWS * block : ROWS * block + ROWS, pl.ds(column, 128)] = source[
                    block ^ j, :, 128 * half : 128 * half + 128
                ].astype(F32)
    own_merged[...] = merged[0:ROWS, :].astype(BF16)
    normed = norm_rows(merged[...]).astype(BF16)
    for half, up in enumerate((up0, up1)):
        columns = slice(512 * half, 512 * half + 512)
        value, rate = gelu_parts(dot(normed, up[...]))
        bundle[:, columns] = value.astype(BF16)
        slope[:, columns] = rate
    bundle[:, 1024:1536] = far_cot[...]


def feed_kernel(bundle, slope, b0, b1, b2, b3, up0, up1, down0, down1, s0, s1, s2, s3):
    cots = stacked_rows((b0, b1, b2, b3), slice(2048, 3072))
    partial, back = 0.0, 0.0
    for half, (up, down) in enumerate(((up0, down0), (up1, down1))):
        columns = slice(512 * half, 512 * half + 512)
        grad = (dot_nt(cots, down[...]) * slope[:, columns]).astype(BF16)
        partial = partial + dot(bundle[:, columns], down[...])
        back = back + dot_nt(grad, up[...])
    for j, sent in enumerate((s0, s1, s2, s3)):
        rows = slice(ROWS * j, ROWS * j + ROWS)
        sent[0] = partial[rows].astype(BF16)
        sent[1] = back[rows].astype(BF16)


def finish_kernel(merged, cot, s0, r1, r2, r3, coarse_out, grad_merged):
    merged_f = merged[...].astype(F32)
    summed = s0[0].astype(F32) + r1[0].astype(F32) + r2[0].astype(F32) + r3[0].astype(F32)
    coarse_out[...] = (merged_f + summed).astype(BF16)
    grad_normed = s0[1].astype(F32) + r1[1].astype(F32) + r2[1].astype(F32) + r3[1].astype(F32)
    centred = merged_f - jnp.mean(merged_f, axis=-1, keepdims=True)
    scale_inv = lax.rsqrt(jnp.mean(centred * centred, axis=-1, keepdims=True) + EPS)
    nhat = centred * scale_inv
    grad = cot[...].astype(F32) + scale_inv * (
        grad_normed
        - jnp.mean(grad_normed, axis=-1, keepdims=True)
        - nhat * jnp.mean(grad_normed * nhat, axis=-1, keepdims=True)
    )
    grad_merged[...] = grad.astype(BF16)


def column_kernel(place, b0, b1, b2, b3, near, far):
    cots = stacked_rows((b0, b1, b2, b3), slice(2048, 3072))
    lat, y, x, zh = place[0], place[1], place[2], place[5]
    source = lax.broadcasted_iota(jnp.int32, (512, 512), 0)
    target = lax.broadcasted_iota(jnp.int32, (512, 512), 1)
    x_part, y_part, z_part = target >> 7, (target >> 5) & 3, (target >> 4) & 1
    x_abs = (x_part ^ (x_part >> 1)) ^ x
    y_abs = (y_part ^ (y_part >> 1)) ^ y
    wanted = (((z_part ^ zh) * 4 + y_abs) * 4 + x_abs) * 16 + (target & 15)
    chosen = jnp.where(source == wanted, 1.0, 0.0).astype(BF16)
    low, high = cots[:, 0:512], cots[:, 512:1024]
    mine = jnp.where(lat == 0, low.astype(F32), high.astype(F32)).astype(BF16)
    theirs = jnp.where(lat == 0, high.astype(F32), low.astype(F32)).astype(BF16)
    near[...] = dot(mine, chosen).astype(BF16)
    far[...] = dot(theirs, chosen).astype(BF16)


def weight_kernel(near, near_hidden, far, kept, s1, s2, s3):
    rows = jnp.concatenate([near[...], far[:, 1024:1536]], axis=0)
    hidden = jnp.concatenate([near_hidden[:, 0:1024], far[:, 0:1024]], axis=0)
    total = dot_tn(rows, hidden)
    kept[...] = total[0:128]
    for part, sent in enumerate((s1, s2, s3)):
        sent[...] = total[128 * part + 128 : 128 * part + 256].astype(BF16)


def plus(kept, *got):
    total = kept[...]
    for g in got:
        total = total + g[...].astype(F32)
    return total


def x_sum_kernel(kept, g1, g2, g3, left, s1, s2, s3):
    total = plus(kept, g1, g2, g3)
    left[...] = total[0:32]
    for part, sent in enumerate((s1, s2, s3)):
        sent[...] = total[32 * part + 32 : 32 * part + 64].astype(BF16)


def y_sum_kernel(kept, g1, g2, g3, left, s1, s2, s3):
    total = plus(kept, g1, g2, g3)
    left[...] = total[0:16, 0:512]
    s1[...] = total[0:16, 512:1024].astype(BF16)
    s2[...] = total[16:32, 0:512].astype(BF16)
    s3[...] = total[16:32, 512:1024].astype(BF16)


def z_sum_kernel(kept, g1, g2, g3, result):
    result[...] = plus(kept, g1, g2, g3)


def token_rows(block):
    return block.transpose(1, 2, 0, 3).reshape(-1, block.shape[-1])


def on_device(fine_tokens, fine_qkv, fine_out, merge_weight, up_weight, down_weight, cotangent):
    lon, tp = lax.axis_index("lon"), lax.axis_index("tp")
    place = jnp.stack(
        [lax.axis_index("lat"), (lon >> 2) & 3, lon & 3, tp >> 2, tp & 3, lon >> 4]
    ).astype(jnp.int32)

    half, two = shaped((160, 512)), shaped((2, 160, 512))
    packed = call(pack_kernel, two, place, merge_weight, up_weight, down_weight, scalars=1)
    packed = along_z(packed)

    own0 = token_rows(fine_tokens[:, :, :3])
    own1 = token_rows(fine_tokens[:, :, 3:])
    west = moved(own1, lambda s: (s + 1) % COUNT)
    east = moved(own0, lambda s: (s - 1) % COUNT)
    cot = jnp.pad(token_rows(cotangent), ((0, ROWS - 36), (0, 0)))

    merged_in = call(
        attend_kernel, shaped((ROWS, 3072)), own0, own1, west, east, fine_qkv, fine_out,
        jnp.asarray(merge_order()), cot, flops=10**9,
    )
    p0, p1 = call(split_kernel, (half, half), packed, after=(merged_in,))
    o0, o1 = ring(p0, 3, 1), ring(p1, 3, -1)
    a0, a1 = call(pair_kernel, (two, two), p0, o0, p1, o1)
    ins = [merged_in] + [swapped(merged_in, j) for j in (1, 2, 3)]
    b0, b1 = ring(a0, 5, 1), ring(a1, 5, -1)
    near = call(four_kernel, shaped((8, 160, 512)), a0, a1, b0, b1, after=ins)
    far_merge, far_up, far_down = call(
        unpack_kernel,
        (shaped((2048, 128)), shaped((1024, 512)), shaped((512, 1024))),
        place, a0, a1, b0, b1, across(near), scalars=1,
    )
    near_cot, far_cot = call(
        column_kernel, (shaped((4 * ROWS, 512)), shaped((4 * ROWS, 512))), place, *ins, scalars=1, flops=10**8
    )

    columns = call(merge_kernel, shaped((4, ROWS, 256)), *ins, merge_weight, far_merge, flops=2 * 10**8)
    held = [columns] + [swapped(columns, j) for j in (1, 2, 3)]

    own_merged, bundle, slope = call(
        hidden_kernel,
        (shaped((ROWS, 1024)), shaped((4 * ROWS, 1536)), shaped((4 * ROWS, 1024), F32)),
        place, *held, up_weight, far_up, far_cot, scalars=1, flops=10**9,
        scratch_shapes=[pltpu.VMEM((4 * ROWS, 1024), F32)],
    )
    other = across(bundle)
    sent = call(
        feed_kernel, tuple(shaped((2, ROWS, 1024)) for _ in range(4)),
        bundle, slope, *ins, up_weight, far_up, down_weight, far_down, flops=2 * 10**9,
    )

    part = shaped((128, 1024))
    kept, *out = call(
        weight_kernel, (shaped((128, 1024), F32), part, part, part), near_cot, bundle, other,
        flops=3 * 10**8, after=sent[1:],
    )
    got = [swapped(o, x_bits(bits)) for o, bits in zip(out, RING[1:])]
    back = [swapped(sent[j], j) for j in (1, 2, 3)]
    part = shaped((32, 1024))
    kept, *out = call(
        x_sum_kernel, (shaped((32, 1024), F32), part, part, part), kept, *got, after=back
    )
    coarse_out, grad_merged = call(
        finish_kernel, (shaped((ROWS, 1024)), shaped((ROWS, 1024))), own_merged, cot, sent[0], *back
    )
    got = [swapped(o, y_bits(bits)) for o, bits in zip(out, RING[1:])]
    part = shaped((16, 512))
    kept, *out = call(
        y_sum_kernel, (shaped((16, 512), F32), part, part, part), kept, *got,
        after=(coarse_out, grad_merged),
    )
    got = [swapped(o, bits) for o, bits in zip(out, (Z_HALF, Z_HI, Z_HALF | Z_HI))]
    grad_down = call(z_sum_kernel, shaped((16, 512), F32), kept, *got).T

    def placed(rows):
        return rows[:36].reshape(6, 3, 2, 1024).transpose(2, 0, 1, 3)

    return placed(coarse_out), placed(grad_merged), grad_down


def solution(mesh):
    tokens = P(None, "lat", ("lon", "tp"), None)
    return jax.shard_map(
        on_device,
        mesh=mesh,
        in_specs=(tokens, P(), P(), P(None, "tp"), P(None, "tp"), P("tp", None), tokens),
        out_specs=(tokens, tokens, P("tp", ("lat", "lon"))),
        check_vma=False,
    )
```

```python
import jax
import jax.numpy as jnp
import numpy as np
from jax import lax
from jax.experimental import pallas as pl
from jax.experimental.pallas import tpu as pltpu
from jax.sharding import Mesh, PartitionSpec as P

EPS = 1e-05
F32 = jnp.float32
BF16 = jnp.bfloat16
AXES = ("lat", "z_hi", "y", "x", "z_half", "z_near")
LINE = AXES[1:]
COUNT = 256
ROWS = 40


def dot(a, b):
    return lax.dot_general(a, b, (((1,), (0,)), ((), ())), preferred_element_type=F32)


def dot_nt(a, b):
    return lax.dot_general(a, b, (((1,), (1,)), ((), ())), preferred_element_type=F32)


def dot_tn(a, b):
    return lax.dot_general(a, b, (((0,), (0,)), ((), ())), preferred_element_type=F32)


def moved(value, target):
    return lax.ppermute(value, LINE, [(s, target(s)) for s in range(COUNT)])


def swapped(value, bits):
    return moved(value, lambda s: s ^ bits)


def across(value):
    return lax.ppermute(value, "lat", [(0, 1), (1, 0)])


def along_z(value):
    pairs = []
    for lat, steps in ((0, 4), (1, -4)):
        for lon in range(32):
            for tp in range(8):
                z = ((lon >> 4) * 8 + tp + steps) % 16
                target = (z >> 3) * 128 + (lon & 15) * 8 + (z & 7)
                pairs.append((lat * COUNT + lon * 8 + tp, lat * COUNT + target))
    return lax.ppermute(value, AXES, pairs)


def exchanged(value, axes):
    return lax.all_to_all(value, axes, 0, 0)


def norm_rows(values):
    centred = values - jnp.mean(values, axis=-1, keepdims=True)
    variance = jnp.mean(centred * centred, axis=-1, keepdims=True)
    return centred * lax.rsqrt(variance + EPS)


def call(kernel, out_shape, *args, flops=0, scalars=0, after=(), **kw):
    specs = [
        pl.BlockSpec(memory_space=pltpu.SMEM if i < scalars else pltpu.VMEM)
        for i in range(len(args))
    ] + [pl.BlockSpec(memory_space=pl.ANY) for _ in after]

    def body(*refs):
        kernel(*refs[: len(args)], *refs[len(args) + len(after) :])

    size = sum(a.size * a.dtype.itemsize for a in args)
    return pl.pallas_call(
        body,
        out_shape=out_shape,
        in_specs=specs,
        out_specs=jax.tree.map(lambda _: pl.BlockSpec(memory_space=pltpu.VMEM), out_shape),
        compiler_params=pltpu.CompilerParams(vmem_limit_bytes=40 * 1024 * 1024),
        cost_estimate=pl.CostEstimate(flops=flops, bytes_accessed=size, transcendentals=0),
        name=kernel.__name__,
        **kw,
    )(*args, *after)


def shaped(shape, dtype=BF16):
    return jax.ShapeDtypeStruct(shape, dtype)


def merge_order():
    order = np.zeros((4 * ROWS, 144), np.float32)
    for quarter in range(4):
        d_lat, d_lon = quarter // 2, quarter % 2
        for token in range(36):
            lat, lon, lev = token // 6, token % 6 // 2, token % 2
            row, column = 2 * lat + d_lat, 2 * lon + d_lon
            source = 72 * (column // 3) + 6 * row + 2 * (column % 3) + lev
            order[ROWS * quarter + token, source] = 1.0
    return order.astype(jnp.bfloat16)


def attend_kernel(own0, own1, west, east, qkv, out_w, order, cot, result):
    tokens = jnp.concatenate(
        [r[...].astype(F32) for r in (own0, own1, west, east)], axis=0
    )
    normed = norm_rows(tokens).astype(BF16)
    packed = dot(normed, qkv[...]).astype(BF16).astype(F32)
    lane = lax.broadcasted_iota(jnp.int32, (1, 128), 1) // 32
    masks = [(lane == h).astype(F32) for h in range(4)]
    scale = 32 ** -0.5
    halves = []
    for window in range(2):
        rows = slice(72 * window, 72 * window + 72)
        other = slice(144 + 72 * window, 216 + 72 * window)
        parts = []
        for group in range(4):
            low = 128 * group
            queries = packed[rows, low : low + 128]
            keys = jnp.concatenate(
                [packed[rows, 512 + low : 640 + low], packed[other, 512 + low : 640 + low]], axis=0
            ).astype(BF16)
            values = jnp.concatenate(
                [packed[rows, 1024 + low : 1152 + low], packed[other, 1024 + low : 1152 + low]], axis=0
            ).astype(BF16)
            stacked = jnp.concatenate([queries * m for m in masks], axis=0).astype(BF16)
            scores = dot_nt(stacked, keys) * scale
            scores = scores - jnp.max(scores, axis=-1, keepdims=True)
            scores = jnp.exp(scores)
            probs = (scores / jnp.sum(scores, axis=-1, keepdims=True)).astype(BF16)
            mixed = dot(probs, values)
            total = mixed[0:72] * masks[0]
            for h in range(1, 4):
                total = total + mixed[72 * h : 72 * h + 72] * masks[h]
            parts.append(total)
        halves.append(jnp.concatenate(parts, axis=1))
    mixed = jnp.concatenate(halves, axis=0).astype(BF16)
    section = (tokens[0:144] + dot(mixed, out_w[...])).astype(BF16)
    spread = dot(order[...], section)
    wide = jnp.concatenate([spread[ROWS * q : ROWS * q + ROWS] for q in range(4)], axis=1)
    merged_in = norm_rows(wide).astype(BF16)
    for copy in range(4):
        result[copy, :, 0:2048] = merged_in
        result[copy, :, 2048:3072] = cot[...]


def stacked_rows(blocks, columns):
    return jnp.concatenate([blocks[j, :, columns].astype(F32) for j in range(4)], axis=0).astype(BF16)


def merge_kernel(ins, own_w, far_w, result):
    blocks = stacked_rows(ins, slice(0, 2048))
    for half, weight in enumerate((own_w, far_w)):
        part = dot(blocks, weight[...]).astype(BF16).astype(F32)
        for j in range(4):
            rows = part[ROWS * j : ROWS * j + ROWS].astype(BF16)
            for copy in range(4):
                result[copy, j, :, 128 * half : 128 * half + 128] = rows


def pack_kernel(place, merge, up, down, packed, done):
    r = place[0] * 16 + place[1] * 4 + place[2]
    row = pl.multiple_of((place[0] * 8 + place[1] * 2 + place[2] // 2) * 32, 32)
    column = pl.multiple_of(lax.rem(place[2], 2) * 512, 512)
    pairs = [
        (up.at[pl.ds(pl.multiple_of(r * 32, 32), 32), :], packed.at[0:32, :]),
        (down.at[pl.ds(row, 32), pl.ds(column, 512)], packed.at[32:64, :]),
    ]
    for q in range(4):
        at = pl.ds(pl.multiple_of(512 * q + r * 16, 16), 16)
        pairs.append((merge.at[at, :], packed.at[64:80, 128 * q : 128 * q + 128]))
    copies = [pltpu.make_async_copy(a, b, done.at[i]) for i, (a, b) in enumerate(pairs)]
    for copy in copies:
        copy.start()
    for copy in copies:
        copy.wait()


def pack(place, merge, up, down):
    hbm = pl.BlockSpec(memory_space=pltpu.HBM)
    return pl.pallas_call(
        pack_kernel,
        out_shape=shaped((80, 512)),
        in_specs=[pl.BlockSpec(memory_space=pltpu.SMEM), hbm, hbm, hbm],
        out_specs=pl.BlockSpec(memory_space=pltpu.VMEM),
        scratch_shapes=[pltpu.SemaphoreType.DMA((6,))],
        name="pack_kernel",
    )(place, merge, up, down)


def spread_kernel(piece, result):
    for copy in range(16):
        result[copy] = piece[...]


def unpack_kernel(place, near, far, merge, up, down):
    for side, source in enumerate((near, far)):
        first = (place[0] ^ side) * 16
        for index in range(16):
            r = first + index
            up[pl.ds(pl.multiple_of(r * 32, 32), 32), :] = source[index, 0:32, :]
            row = pl.multiple_of((first + index - index % 2) * 16, 32)
            column = 512 * (index % 2)
            down[pl.ds(row, 32), column : column + 512] = source[index, 32:64, :]
            for q in range(4):
                at = pl.multiple_of(512 * q + r * 16, 16)
                merge[pl.ds(at, 16), :] = source[index, 64:80, 128 * q : 128 * q + 128]


def gelu_parts(values):
    cdf = 0.5 * (1.0 + lax.erf(values * np.float32(np.sqrt(0.5))))
    density = jnp.exp(-0.5 * values * values) * np.float32(1.0 / np.sqrt(2.0 * np.pi))
    return values * cdf, cdf + values * density


def hidden_kernel(place, columns, ins, up0, up1, own_merged, bundle, slope, merged):
    lat, half_index, near = place[0], place[3], place[4]
    for j in range(4):
        for half in range(2):
            column = pl.multiple_of(((half_index ^ half) * 4 + j) * 128, 128)
            for block in range(4):
                merged[ROWS * block : ROWS * block + ROWS, pl.ds(column, 128)] = columns[
                    j, block, :, 128 * half : 128 * half + 128
                ].astype(F32)
    own_merged[...] = merged[pl.ds(pl.multiple_of(near * ROWS, 8), ROWS), :].astype(BF16)
    normed = norm_rows(merged[...]).astype(BF16)
    for half, up in enumerate((up0, up1)):
        at = slice(512 * half, 512 * half + 512)
        value, rate = gelu_parts(dot(normed, up[...]))
        bundle[:, at] = value.astype(BF16)
        slope[:, at] = rate
    at = pl.ds(pl.multiple_of(2048 + (1 - lat) * 512, 512), 512)
    bundle[:, 1024:1536] = stacked_rows(ins, at)


def feed_kernel(place, bundle, slope, ins, up0, up1, down0, down1, kept, sent, partial, back):
    cots = stacked_rows(ins, slice(2048, 3072))
    values, grads = 0.0, 0.0
    for half, (up, down) in enumerate(((up0, down0), (up1, down1))):
        at = slice(512 * half, 512 * half + 512)
        grad = (dot_nt(cots, down[...]) * slope[:, at]).astype(BF16)
        values = values + dot(bundle[:, at], down[...])
        grads = grads + dot_nt(grad, up[...])
    partial[...] = values
    back[...] = grads
    for j in range(4):
        rows = pl.ds(pl.multiple_of((place[4] ^ j) * ROWS, 8), ROWS)
        for index, source in enumerate((partial, back)):
            if j < 2:
                kept[j, index] = source[rows, :]
            else:
                sent[j - 2, index] = source[rows, :].astype(BF16)


def halve_kernel(kept, got, left, sent):
    left[...] = kept[0] + got[0].astype(F32)
    sent[...] = (kept[1] + got[1].astype(F32)).astype(BF16)


def finish_kernel(merged, cot, left, got, coarse_out, grad_merged):
    merged_f = merged[...].astype(F32)
    coarse_out[...] = (merged_f + left[0] + got[0].astype(F32)).astype(BF16)
    grad_normed = left[1] + got[1].astype(F32)
    centred = merged_f - jnp.mean(merged_f, axis=-1, keepdims=True)
    scale_inv = lax.rsqrt(jnp.mean(centred * centred, axis=-1, keepdims=True) + EPS)
    nhat = centred * scale_inv
    grad = cot[...].astype(F32) + scale_inv * (
        grad_normed
        - jnp.mean(grad_normed, axis=-1, keepdims=True)
        - nhat * jnp.mean(grad_normed * nhat, axis=-1, keepdims=True)
    )
    grad_merged[...] = grad.astype(BF16)


def weight_kernel(place, ins, bundle, other, result):
    at = pl.ds(pl.multiple_of(2048 + place[0] * 512, 512), 512)
    rows = jnp.concatenate([stacked_rows(ins, at), other[:, 1024:1536]], axis=0)
    hidden = jnp.concatenate([bundle[:, 0:1024], other[:, 0:1024]], axis=0)
    total = dot_tn(rows, hidden)
    for z_hi in range(2):
        for index in range(16):
            low = 256 * z_hi + 16 * index
            result[index, 16 * z_hi : 16 * z_hi + 16, :] = total[low : low + 16].astype(BF16)


def plane_sum_kernel(place, parts, result, total):
    summed = parts[0].astype(F32)
    for index in range(1, 16):
        summed = summed + parts[index].astype(F32)
    total[...] = summed
    for z_hi in range(2):
        for half in range(2):
            at = pl.ds(pl.multiple_of((place[3] ^ half) * 512, 512), 512)
            result[2 * z_hi + half] = total[16 * z_hi : 16 * z_hi + 16, at].astype(BF16)


def line_sum_kernel(parts, result):
    summed = parts[0].astype(F32)
    for index in range(1, 4):
        summed = summed + parts[index].astype(F32)
    result[...] = summed


def token_rows(block):
    return block.transpose(1, 2, 0, 3).reshape(-1, block.shape[-1])


def on_device(fine_tokens, fine_qkv, fine_out, merge_weight, up_weight, down_weight, cotangent):
    place = jnp.stack([lax.axis_index(a) for a in ("lat", "y", "x", "z_half", "z_near")]).astype(jnp.int32)

    own0 = token_rows(fine_tokens[:, :, :3])
    own1 = token_rows(fine_tokens[:, :, 3:])
    west = moved(own1, lambda s: (s + 1) % COUNT)
    east = moved(own0, lambda s: (s - 1) % COUNT)
    cot = jnp.pad(token_rows(cotangent), ((0, ROWS - 36), (0, 0)))

    piece = along_z(pack(place, merge_weight, up_weight, down_weight))
    near = exchanged(call(spread_kernel, shaped((16, 80, 512)), piece), ("y", "x"))
    far = across(near)

    merged_in = call(
        attend_kernel, shaped((4, ROWS, 3072)), own0, own1, west, east, fine_qkv, fine_out,
        jnp.asarray(merge_order()), cot, flops=10**9, after=(near,),
    )
    ins = exchanged(merged_in, "z_near")
    far_merge, far_up, far_down = call(
        unpack_kernel,
        (shaped((2048, 128)), shaped((1024, 512)), shaped((512, 1024))),
        place, near, far, scalars=1, after=(ins,),
    )
    columns = call(merge_kernel, shaped((4, 4, ROWS, 256)), ins, merge_weight, far_merge, flops=2 * 10**8)
    columns = exchanged(columns, "z_near")
    own_merged, bundle, slope = call(
        hidden_kernel,
        (shaped((ROWS, 1024)), shaped((4 * ROWS, 1536)), shaped((4 * ROWS, 1024), F32)),
        place, columns, ins, up_weight, far_up, scalars=1, flops=10**9,
        scratch_shapes=[pltpu.VMEM((4 * ROWS, 1024), F32)],
    )
    other = across(bundle)
    kept, sent = call(
        feed_kernel, (shaped((2, 2, ROWS, 1024), F32), shaped((2, 2, ROWS, 1024))),
        place, bundle, slope, ins, up_weight, far_up, down_weight, far_down, scalars=1, flops=2 * 10**9,
        scratch_shapes=[pltpu.VMEM((4 * ROWS, 1024), F32)] * 2,
    )
    got = swapped(sent, 2)

    parts = call(
        weight_kernel, shaped((16, 32, 1024)), place, ins, bundle, other, scalars=1,
        flops=3 * 10**8, after=(sent,),
    )
    parts = exchanged(parts, ("y", "x"))
    left, sent = call(
        halve_kernel, (shaped((2, ROWS, 1024), F32), shaped((2, ROWS, 1024))), kept, got, after=(parts,)
    )
    got = swapped(sent, 1)
    parts = call(
        plane_sum_kernel, shaped((4, 16, 512)), place, parts, scalars=1,
        scratch_shapes=[pltpu.VMEM((32, 1024), F32)], after=(sent,),
    )
    parts = exchanged(parts, ("z_hi", "z_half"))
    coarse_out, grad_merged = call(
        finish_kernel, (shaped((ROWS, 1024)), shaped((ROWS, 1024))), own_merged, cot, left, got,
        after=(parts,),
    )
    grad_down = call(line_sum_kernel, shaped((16, 512), F32), parts).T

    def placed(rows):
        return rows[:36].reshape(6, 3, 2, 1024).transpose(2, 0, 1, 3)

    return placed(coarse_out), placed(grad_merged), grad_down


def solution(mesh):
    lon, tp = ("z_hi", "y", "x"), ("z_half", "z_near")
    parts = Mesh(mesh.devices.reshape(2, 2, 4, 4, 2, 4), AXES)
    tokens = P(None, "lat", lon + tp, None)
    return jax.shard_map(
        on_device,
        mesh=parts,
        in_specs=(tokens, P(), P(), P(None, tp), P(None, tp), P(tp, None), tokens),
        out_specs=(tokens, tokens, P(tp, ("lat",) + lon)),
        check_vma=False,
    )
```

```python
import jax
import jax.numpy as jnp
import numpy as np
from jax import lax
from jax.experimental import pallas as pl
from jax.experimental.pallas import tpu as pltpu
from jax.sharding import Mesh, PartitionSpec as P

EPS = 1e-05
F32 = jnp.float32
BF16 = jnp.bfloat16
AXES = ("lat", "z_hi", "y", "x", "z_half", "z_near")
LINE = AXES[1:]
COUNT = 256
ROWS = 40


def dot(a, b):
    return lax.dot_general(a, b, (((1,), (0,)), ((), ())), preferred_element_type=F32)


def dot_nt(a, b):
    return lax.dot_general(a, b, (((1,), (1,)), ((), ())), preferred_element_type=F32)


def dot_tn(a, b):
    return lax.dot_general(a, b, (((0,), (0,)), ((), ())), preferred_element_type=F32)


def moved(value, target):
    return lax.ppermute(value, LINE, [(s, target(s)) for s in range(COUNT)])


def swapped(value, bits):
    return moved(value, lambda s: s ^ bits)


def across(value):
    return lax.ppermute(value, "lat", [(0, 1), (1, 0)])


def along_z(value):
    pairs = []
    for lat, steps in ((0, 4), (1, -4)):
        for lon in range(32):
            for tp in range(8):
                z = ((lon >> 4) * 8 + tp + steps) % 16
                target = (z >> 3) * 128 + (lon & 15) * 8 + (z & 7)
                pairs.append((lat * COUNT + lon * 8 + tp, lat * COUNT + target))
    return lax.ppermute(value, AXES, pairs)


def exchanged(value, axes):
    return lax.all_to_all(value, axes, 0, 0)


def norm_rows(values):
    centred = values - jnp.mean(values, axis=-1, keepdims=True)
    variance = jnp.mean(centred * centred, axis=-1, keepdims=True)
    return centred * lax.rsqrt(variance + EPS)


def call(kernel, out_shape, *args, flops=0, scalars=0, after=(), **kw):
    specs = [
        pl.BlockSpec(memory_space=pltpu.SMEM if i < scalars else pltpu.VMEM)
        for i in range(len(args))
    ] + [pl.BlockSpec(memory_space=pl.ANY) for _ in after]

    def body(*refs):
        kernel(*refs[: len(args)], *refs[len(args) + len(after) :])

    size = sum(a.size * a.dtype.itemsize for a in args)
    return pl.pallas_call(
        body,
        out_shape=out_shape,
        in_specs=specs,
        out_specs=jax.tree.map(lambda _: pl.BlockSpec(memory_space=pltpu.VMEM), out_shape),
        compiler_params=pltpu.CompilerParams(vmem_limit_bytes=16 * 1024 * 1024),
        cost_estimate=pl.CostEstimate(flops=flops, bytes_accessed=size, transcendentals=0),
        name=kernel.__name__,
        **kw,
    )(*args, *after)


def shaped(shape, dtype=BF16):
    return jax.ShapeDtypeStruct(shape, dtype)


def merge_order():
    order = np.zeros((4 * ROWS, 144), np.float32)
    for quarter in range(4):
        d_lat, d_lon = quarter // 2, quarter % 2
        for token in range(36):
            lat, lon, lev = token // 6, token % 6 // 2, token % 2
            row, column = 2 * lat + d_lat, 2 * lon + d_lon
            source = 72 * (column // 3) + 6 * row + 2 * (column % 3) + lev
            order[ROWS * quarter + token, source] = 1.0
    return order.astype(jnp.bfloat16)


def attend_kernel(own0, own1, west, east, qkv, out_w, order, result):
    tokens = jnp.concatenate(
        [r[...].astype(F32) for r in (own0, own1, west, east)], axis=0
    )
    normed = norm_rows(tokens).astype(BF16)
    packed = dot(normed, qkv[...]).astype(BF16).astype(F32)
    lane = lax.broadcasted_iota(jnp.int32, (1, 128), 1) // 32
    masks = [(lane == h).astype(F32) for h in range(4)]
    scale = 32 ** -0.5
    halves = []
    for window in range(2):
        rows = slice(72 * window, 72 * window + 72)
        other = slice(144 + 72 * window, 216 + 72 * window)
        parts = []
        for group in range(4):
            low = 128 * group
            queries = packed[rows, low : low + 128]
            keys = jnp.concatenate(
                [packed[rows, 512 + low : 640 + low], packed[other, 512 + low : 640 + low]], axis=0
            ).astype(BF16)
            values = jnp.concatenate(
                [packed[rows, 1024 + low : 1152 + low], packed[other, 1024 + low : 1152 + low]], axis=0
            ).astype(BF16)
            stacked = jnp.concatenate([queries * m for m in masks], axis=0).astype(BF16)
            scores = dot_nt(stacked, keys) * scale
            scores = scores - jnp.max(scores, axis=-1, keepdims=True)
            scores = jnp.exp(scores)
            probs = (scores / jnp.sum(scores, axis=-1, keepdims=True)).astype(BF16)
            mixed = dot(probs, values)
            total = mixed[0:72] * masks[0]
            for h in range(1, 4):
                total = total + mixed[72 * h : 72 * h + 72] * masks[h]
            parts.append(total)
        halves.append(jnp.concatenate(parts, axis=1))
    mixed = jnp.concatenate(halves, axis=0).astype(BF16)
    section = (tokens[0:144] + dot(mixed, out_w[...])).astype(BF16)
    spread = dot(order[...], section)
    wide = jnp.concatenate([spread[ROWS * q : ROWS * q + ROWS] for q in range(4)], axis=1)
    merged_in = norm_rows(wide).astype(BF16)
    for copy in range(4):
        result[copy] = merged_in


def stacked_rows(blocks, columns):
    return jnp.concatenate([blocks[j, :, columns].astype(F32) for j in range(4)], axis=0).astype(BF16)


def merge_kernel(ins, own_w, far_w, result):
    blocks = stacked_rows(ins, slice(0, 2048))
    for half, weight in enumerate((own_w, far_w)):
        part = dot(blocks, weight[...]).astype(BF16).astype(F32)
        for j in range(4):
            rows = part[ROWS * j : ROWS * j + ROWS].astype(BF16)
            for copy in range(4):
                result[copy, j, :, 128 * half : 128 * half + 128] = rows


def prepare_kernel(
    place, tokens, cotangent, merge, up, down, west_side, east_side, packed, cot, tokens_in, cot_in, done
):
    r = place[0] * 16 + place[1] * 4 + place[2]
    row = pl.multiple_of((place[0] * 8 + place[1] * 2 + place[2] // 2) * 32, 32)
    column = pl.multiple_of(lax.rem(place[2], 2) * 512, 512)
    pairs = [
        (tokens, tokens_in),
        (cotangent, cot_in),
        (up.at[pl.ds(pl.multiple_of(r * 32, 32), 32), :], packed.at[0:32, :]),
        (down.at[pl.ds(row, 32), pl.ds(column, 512)], packed.at[32:64, :]),
    ]
    for q in range(4):
        at = pl.ds(pl.multiple_of(512 * q + r * 16, 16), 16)
        pairs.append((merge.at[at, :], packed.at[64:80, 128 * q : 128 * q + 128]))
    copies = [pltpu.make_async_copy(a, b, done.at[i]) for i, (a, b) in enumerate(pairs)]
    for copy in copies:
        copy.start()
    copies[0].wait()
    for lat in range(12):
        for lon in range(3):
            rows = slice(6 * lat + 2 * lon, 6 * lat + 2 * lon + 2)
            west_side[rows, :] = tokens_in[lat, lon]
            east_side[rows, :] = tokens_in[lat, lon + 3]
    copies[1].wait()
    for copy in range(4):
        for lat in range(6):
            for lon in range(3):
                cot[copy, 6 * lat + 2 * lon : 6 * lat + 2 * lon + 2, :] = cot_in[lat, lon]
        cot[copy, 36:40, :] = jnp.zeros((4, 1024), BF16)
    for copy in copies[2:]:
        copy.wait()


def prepare(place, tokens, cotangent, merge, up, down):
    hbm = pl.BlockSpec(memory_space=pltpu.HBM)
    vmem = pl.BlockSpec(memory_space=pltpu.VMEM)
    return pl.pallas_call(
        prepare_kernel,
        out_shape=(shaped((72, 512)), shaped((72, 512)), shaped((80, 512)), shaped((4, ROWS, 1024))),
        in_specs=[pl.BlockSpec(memory_space=pltpu.SMEM), hbm, hbm, hbm, hbm, hbm],
        out_specs=(vmem,) * 4,
        scratch_shapes=[
            pltpu.VMEM((12, 6, 2, 512), BF16),
            pltpu.VMEM((6, 3, 2, 1024), BF16),
            pltpu.SemaphoreType.DMA((8,)),
        ],
        name="prepare_kernel",
    )(place, tokens.transpose(1, 2, 0, 3), cotangent.transpose(1, 2, 0, 3), merge, up, down)


def spread_kernel(piece, result):
    for copy in range(16):
        result[copy] = piece[...]


def unpack_kernel(place, near, far, merge, up, down):
    for side, source in enumerate((near, far)):
        first = (place[0] ^ side) * 16
        for index in range(16):
            r = first + index
            up[pl.ds(pl.multiple_of(r * 32, 32), 32), :] = source[index, 0:32, :]
            row = pl.multiple_of((first + index - index % 2) * 16, 32)
            column = 512 * (index % 2)
            down[pl.ds(row, 32), column : column + 512] = source[index, 32:64, :]
            for q in range(4):
                at = pl.multiple_of(512 * q + r * 16, 16)
                merge[pl.ds(at, 16), :] = source[index, 64:80, 128 * q : 128 * q + 128]


def gelu_parts(values):
    cdf = 0.5 * (1.0 + lax.erf(values * np.float32(np.sqrt(0.5))))
    density = jnp.exp(-0.5 * values * values) * np.float32(1.0 / np.sqrt(2.0 * np.pi))
    return values * cdf, cdf + values * density


def hidden_kernel(place, columns, cots, up0, up1, own_merged, bundle, slope, merged):
    lat, half_index, near = place[0], place[3], place[4]
    for j in range(4):
        for half in range(2):
            column = pl.multiple_of(((half_index ^ half) * 4 + j) * 128, 128)
            for block in range(4):
                merged[ROWS * block : ROWS * block + ROWS, pl.ds(column, 128)] = columns[
                    j, block, :, 128 * half : 128 * half + 128
                ].astype(F32)
    own_merged[...] = merged[pl.ds(pl.multiple_of(near * ROWS, 8), ROWS), :].astype(BF16)
    normed = norm_rows(merged[...]).astype(BF16)
    for half, up in enumerate((up0, up1)):
        at = slice(512 * half, 512 * half + 512)
        value, rate = gelu_parts(dot(normed, up[...]))
        bundle[:, at] = value.astype(BF16)
        slope[:, at] = rate
    at = pl.ds(pl.multiple_of((1 - lat) * 512, 512), 512)
    bundle[:, 1024:1536] = stacked_rows(cots, at)


def feed_kernel(bundle, slope, cots, up0, up1, down0, down1, sent):
    cots = stacked_rows(cots, slice(0, 1024))
    values, grads = 0.0, 0.0
    for half, (up, down) in enumerate(((up0, down0), (up1, down1))):
        at = slice(512 * half, 512 * half + 512)
        grad = (dot_nt(cots, down[...]) * slope[:, at]).astype(BF16)
        values = values + dot(bundle[:, at], down[...])
        grads = grads + dot_nt(grad, up[...])
    for j in range(4):
        rows = slice(ROWS * j, ROWS * j + ROWS)
        sent[j, 0] = values[rows].astype(BF16)
        sent[j, 1] = grads[rows].astype(BF16)


def finish_kernel(merged, cot, got, coarse_out, grad_merged):
    merged_f = merged[...].astype(F32)
    summed = got[0].astype(F32)
    for j in range(1, 4):
        summed = summed + got[j].astype(F32)
    value = (merged_f + summed[0]).astype(BF16)
    grad_normed = summed[1]
    centred = merged_f - jnp.mean(merged_f, axis=-1, keepdims=True)
    scale_inv = lax.rsqrt(jnp.mean(centred * centred, axis=-1, keepdims=True) + EPS)
    nhat = centred * scale_inv
    grad = cot[0].astype(F32) + scale_inv * (
        grad_normed
        - jnp.mean(grad_normed, axis=-1, keepdims=True)
        - nhat * jnp.mean(grad_normed * nhat, axis=-1, keepdims=True)
    )
    grad = grad.astype(BF16)
    for lat in range(6):
        for lon in range(3):
            rows = slice(6 * lat + 2 * lon, 6 * lat + 2 * lon + 2)
            coarse_out[lat, lon] = value[rows]
            grad_merged[lat, lon] = grad[rows]


def weight_kernel(place, cots, bundle, other, result):
    at = pl.ds(pl.multiple_of(place[0] * 512, 512), 512)
    rows = jnp.concatenate([stacked_rows(cots, at), other[:, 1024:1536]], axis=0)
    hidden = jnp.concatenate([bundle[:, 0:1024], other[:, 0:1024]], axis=0)
    total = dot_tn(rows, hidden)
    for z_hi in range(2):
        for index in range(16):
            low = 256 * z_hi + 16 * index
            result[index, 16 * z_hi : 16 * z_hi + 16, :] = total[low : low + 16].astype(BF16)


def plane_sum_kernel(place, parts, result, total):
    summed = parts[0].astype(F32)
    for index in range(1, 16):
        summed = summed + parts[index].astype(F32)
    total[...] = summed
    for z_hi in range(2):
        for half in range(2):
            at = pl.ds(pl.multiple_of((place[3] ^ half) * 512, 512), 512)
            result[2 * z_hi + half] = total[16 * z_hi : 16 * z_hi + 16, at].astype(BF16)


def line_sum_kernel(parts, result):
    summed = parts[0].astype(F32)
    for index in range(1, 4):
        summed = summed + parts[index].astype(F32)
    result[...] = summed


def on_device(fine_tokens, fine_qkv, fine_out, merge_weight, up_weight, down_weight, cotangent):
    place = jnp.stack([lax.axis_index(a) for a in ("lat", "y", "x", "z_half", "z_near")]).astype(jnp.int32)
    own0, own1, piece, cot = prepare(place, fine_tokens, cotangent, merge_weight, up_weight, down_weight)

    west = moved(own1, lambda s: (s + 1) % COUNT)
    east = moved(own0, lambda s: (s - 1) % COUNT)
    piece = along_z(piece)
    cots = exchanged(cot, "z_near")

    pieces = call(spread_kernel, shaped((16, 80, 512)), piece, after=(west, east, cots))
    near = exchanged(pieces, ("y", "x"))
    far = across(near)
    merged_in = call(
        attend_kernel, shaped((4, ROWS, 2048)), own0, own1, west, east, fine_qkv, fine_out,
        jnp.asarray(merge_order()), flops=10**9, after=(pieces,),
    )
    ins = exchanged(merged_in, "z_near")
    far_merge, far_up, far_down = call(
        unpack_kernel,
        (shaped((2048, 128)), shaped((1024, 512)), shaped((512, 1024))),
        place, near, far, scalars=1, after=(ins,),
    )
    columns = call(merge_kernel, shaped((4, 4, ROWS, 256)), ins, merge_weight, far_merge, flops=2 * 10**8)
    columns = exchanged(columns, "z_near")
    own_merged, bundle, slope = call(
        hidden_kernel,
        (shaped((ROWS, 1024)), shaped((4 * ROWS, 1536)), shaped((4 * ROWS, 1024), F32)),
        place, columns, cots, up_weight, far_up, scalars=1, flops=10**9,
        scratch_shapes=[pltpu.VMEM((4 * ROWS, 1024), F32)],
    )
    other = across(bundle)
    partials = call(
        feed_kernel, shaped((4, 2, ROWS, 1024)),
        bundle, slope, cots, up_weight, far_up, down_weight, far_down, flops=2 * 10**9,
    )
    parts = call(
        weight_kernel, shaped((16, 32, 1024)), place, cots, bundle, other, scalars=1,
        flops=3 * 10**8, after=(partials,),
    )
    parts = exchanged(parts, ("y", "x"))
    got = exchanged(partials, "z_near")
    parts = call(
        plane_sum_kernel, shaped((4, 16, 512)), place, parts, scalars=1,
        scratch_shapes=[pltpu.VMEM((32, 1024), F32)],
    )
    parts = exchanged(parts, ("z_hi", "z_half"))
    tokens = shaped((6, 3, 2, 1024))
    coarse_out, grad_merged = call(finish_kernel, (tokens, tokens), own_merged, cot, got)
    grad_down = call(
        line_sum_kernel, shaped((16, 512), F32), parts, after=(coarse_out, grad_merged)
    ).T
    return coarse_out.transpose(2, 0, 1, 3), grad_merged.transpose(2, 0, 1, 3), grad_down


def solution(mesh):
    lon, tp = ("z_hi", "y", "x"), ("z_half", "z_near")
    parts = Mesh(mesh.devices.reshape(2, 2, 4, 4, 2, 4), AXES)
    tokens = P(None, "lat", lon + tp, None)
    return jax.shard_map(
        on_device,
        mesh=parts,
        in_specs=(tokens, P(), P(), P(None, tp), P(None, tp), P(tp, None), tokens),
        out_specs=(tokens, tokens, P(tp, ("lat",) + lon)),
        check_vma=False,
    )
```

```python
import jax
import jax.numpy as jnp
import numpy as np
from jax import lax
from jax.experimental import pallas as pl
from jax.experimental.pallas import tpu as pltpu
from jax.sharding import Mesh, PartitionSpec as P

EPS = 1e-05
F32 = jnp.float32
BF16 = jnp.bfloat16
AXES = ("lat", "z_hi", "y", "x", "z_half", "z_near")
LINE = AXES[1:]
COUNT = 256
ROWS = 40


def dot(a, b):
    return lax.dot_general(a, b, (((1,), (0,)), ((), ())), preferred_element_type=F32)


def dot_nt(a, b):
    return lax.dot_general(a, b, (((1,), (1,)), ((), ())), preferred_element_type=F32)


def dot_tn(a, b):
    return lax.dot_general(a, b, (((0,), (0,)), ((), ())), preferred_element_type=F32)


def moved(value, target):
    return lax.ppermute(value, LINE, [(s, target(s)) for s in range(COUNT)])


def swapped(value, bits):
    return moved(value, lambda s: s ^ bits)


def across(value):
    return lax.ppermute(value, "lat", [(0, 1), (1, 0)])


def along_z(value):
    pairs = []
    for lat, steps in ((0, 4), (1, -4)):
        for lon in range(32):
            for tp in range(8):
                z = ((lon >> 4) * 8 + tp + steps) % 16
                target = (z >> 3) * 128 + (lon & 15) * 8 + (z & 7)
                pairs.append((lat * COUNT + lon * 8 + tp, lat * COUNT + target))
    return lax.ppermute(value, AXES, pairs)


def exchanged(value, axes):
    return lax.all_to_all(value, axes, 0, 0)


def norm_rows(values):
    centred = values - jnp.mean(values, axis=-1, keepdims=True)
    variance = jnp.mean(centred * centred, axis=-1, keepdims=True)
    return centred * lax.rsqrt(variance + EPS)


def in_hbm(value):
    return pltpu.with_memory_space_constraint(value, pltpu.HBM)


def call(kernel, out_shape, *args, flops=0, scalars=0, hbm=(), hbm_out=0, after=(), through=(), limit=16, **kw):
    outs = out_shape if isinstance(out_shape, tuple) else (out_shape,)
    here, far = pl.BlockSpec(memory_space=pltpu.VMEM), pl.BlockSpec(memory_space=pltpu.HBM)
    scalar = pl.BlockSpec(memory_space=pltpu.SMEM)
    specs = [scalar if i < scalars else far if i in hbm else here for i in range(len(args))]
    first, last = len(args) + len(after), len(args) + len(after) + len(through)

    def body(*refs):
        kernel(*refs[: len(args)], *refs[last : last + len(outs)], *refs[last + len(outs) + len(through) :])

    size = sum(a.size * a.dtype.itemsize for a in args)
    result = pl.pallas_call(
        body,
        out_shape=tuple(pltpu.HBM(o.shape, o.dtype) if i < hbm_out else o for i, o in enumerate(outs))
        + tuple(pltpu.HBM(t.shape, t.dtype) for t in through),
        in_specs=specs + [far] * (len(after) + len(through)),
        out_specs=(far,) * hbm_out + (here,) * (len(outs) - hbm_out) + (far,) * len(through),
        input_output_aliases={first + i: len(outs) + i for i in range(len(through))},
        compiler_params=pltpu.CompilerParams(vmem_limit_bytes=limit * 1024 * 1024) if limit else None,
        cost_estimate=pl.CostEstimate(flops=flops, bytes_accessed=size, transcendentals=0),
        name=kernel.__name__,
        **kw,
    )(*(in_hbm(a) if i in hbm else a for i, a in enumerate(args)), *(in_hbm(a) for a in (*after, *through)))
    return result if len(result) > 1 else result[0]


def shaped(shape, dtype=BF16):
    return jax.ShapeDtypeStruct(shape, dtype)


def merge_order():
    order = np.zeros((2, 4 * ROWS, 144), np.float32)
    for odd in range(2):
        for quarter in range(4):
            d_lat, d_lon = quarter // 2, quarter % 2
            for token in range(36):
                lat, lon, lev = token // 6, token % 6 // 2, token % 2
                row, column = 2 * lat + d_lat, 2 * lon + d_lon
                side = column // 3 if odd else 1 - column // 3
                order[odd, ROWS * quarter + token, 72 * side + 6 * row + 2 * (column % 3) + lev] = 1.0
    return order.astype(jnp.bfloat16)


def started(copies):
    copies = [pltpu.make_async_copy(*c) for c in copies]
    for copy in copies:
        copy.start()
    return copies


def project_kernel(side0, side1, qkv, packed):
    tokens = jnp.concatenate([side0[...].astype(F32), side1[0:72].astype(F32)], axis=0)
    packed[...] = dot(norm_rows(tokens).astype(BF16), qkv[...]).astype(BF16)


def attend_kernel(place, side0, side1, own, got0, got1, qkv, out_w, order, result, merged_in, done):
    tokens = jnp.concatenate([side0[...].astype(F32), side1[0:72].astype(F32)], axis=0)
    others = jnp.concatenate([got0[...].astype(F32), got1[0:72].astype(F32)], axis=0)
    other_packed = dot(norm_rows(others).astype(BF16), qkv[:, 512:1536]).astype(BF16).astype(F32)
    packed = own[...].astype(F32)
    lane = lax.broadcasted_iota(jnp.int32, (1, 128), 1) // 32
    masks = [(lane == h).astype(F32) for h in range(4)]
    scale = 32 ** -0.5
    halves = []
    for window in range(2):
        rows = slice(72 * window, 72 * window + 72)
        parts = []
        for group in range(4):
            low = 128 * group
            queries = packed[rows, low : low + 128]
            keys = jnp.concatenate(
                [packed[rows, 512 + low : 640 + low], other_packed[rows, low : low + 128]], axis=0
            ).astype(BF16)
            values = jnp.concatenate(
                [packed[rows, 1024 + low : 1152 + low], other_packed[rows, 512 + low : 640 + low]], axis=0
            ).astype(BF16)
            stacked = jnp.concatenate([queries * m for m in masks], axis=0).astype(BF16)
            scores = dot_nt(stacked, keys) * scale
            scores = scores - jnp.max(scores, axis=-1, keepdims=True)
            scores = jnp.exp(scores)
            probs = (scores / jnp.sum(scores, axis=-1, keepdims=True)).astype(BF16)
            mixed = dot(probs, values)
            total = mixed[0:72] * masks[0]
            for h in range(1, 4):
                total = total + mixed[72 * h : 72 * h + 72] * masks[h]
            parts.append(total)
        halves.append(jnp.concatenate(parts, axis=1))
    mixed = jnp.concatenate(halves, axis=0).astype(BF16)
    section = (tokens + dot(mixed, out_w[...])).astype(BF16)
    spread = dot(order[place[4] & 1], section)
    wide = jnp.concatenate([spread[ROWS * q : ROWS * q + ROWS] for q in range(4)], axis=1)
    merged_in[...] = norm_rows(wide).astype(BF16)
    for copy in started([(merged_in, result, done)]):
        copy.wait()


def stacked_rows(blocks, columns):
    return jnp.concatenate([blocks[j, :, columns].astype(F32) for j in range(4)], axis=0).astype(BF16)


def merge_half(place, source, side, weight):
    for index in range(16):
        for q in range(4):
            weight[64 * index + 16 * q : 64 * index + 16 * q + 16, :] = source[index, 64:80, 128 * q : 128 * q + 128]
    return pl.ds(pl.multiple_of((place[0] ^ side) * 1024, 1024), 1024)


def merge_near_kernel(place, b0, b1, b2, b3, own_w, near, rows, own, part, blocks, weight, done):
    copies = started([(block, blocks.at[j], done.at[j]) for j, block in enumerate((b0, b1, b2, b3))])
    at = merge_half(place, near, 0, weight)
    for copy in copies:
        copy.wait()
    rows[...] = jnp.concatenate([blocks[j].astype(F32) for j in range(4)], axis=0).astype(BF16)
    own[...] = dot(rows[...], own_w[...])
    part[...] = dot(rows[:, at], weight[...])


def merge_kernel(place, rows, own, part, far, result, weight):
    at = merge_half(place, far, 1, weight)
    for half, part in enumerate((own[...], part[...] + dot(rows[:, at], weight[...]))):
        for j in range(4):
            piece = part[ROWS * j : ROWS * j + ROWS].astype(BF16)
            for copy in range(4):
                result[copy, place[4] ^ j, :, 128 * half : 128 * half + 128] = piece


def prepare_kernel(
    tokens, cotangent, merge, up, down, side0, side1, packed, cot, tokens_in, cot_in, done
):
    r = lax.axis_index("lat") * 16 + lax.axis_index("y") * 4 + lax.axis_index("x")
    east = 1 - (lax.axis_index("z_near") & 1)
    pairs = [
        (tokens, tokens_in),
        (cotangent, cot_in),
        (up.at[pl.ds(pl.multiple_of(r * 32, 32), 32), :], packed.at[0:32, :]),
    ]
    row = pl.ds(pl.multiple_of(r * 16, 16), 16)
    for half in range(2):
        pairs.append((down.at[row, 512 * half : 512 * half + 512], packed.at[32 + 16 * half : 48 + 16 * half, :]))
    for q in range(4):
        at = pl.ds(pl.multiple_of(r * 64 + 16 * q, 16), 16)
        pairs.append((merge.at[at, :], packed.at[64:80, 128 * q : 128 * q + 128]))
    copies = started([(a, b, done.at[i]) for i, (a, b) in enumerate(pairs)])
    copies[0].wait()
    for lat in range(12):
        for lon in range(3):
            rows = slice(6 * lat + 2 * lon, 6 * lat + 2 * lon + 2)
            side0[rows, :] = tokens_in[lat, 3 * east + lon]
            side1[rows, :] = tokens_in[lat, 3 * (1 - east) + lon]
    side1[72:96, :] = jnp.zeros((24, 512), BF16)
    copies[1].wait()
    for copy in range(4):
        for lat in range(6):
            for lon in range(3):
                cot[copy, 6 * lat + 2 * lon : 6 * lat + 2 * lon + 2, :] = cot_in[lat, lon]
        cot[copy, 36:40, :] = jnp.zeros((4, 1024), BF16)
    for copy in copies[2:]:
        copy.wait()


def prepare(tokens, cotangent, merge, up, down):
    hbm = pl.BlockSpec(memory_space=pltpu.HBM)
    vmem = pl.BlockSpec(memory_space=pltpu.VMEM)
    return pl.pallas_call(
        prepare_kernel,
        out_shape=(shaped((72, 512)), shaped((96, 512)), shaped((80, 512)), shaped((4, ROWS, 1024))),
        in_specs=[hbm] * 5,
        out_specs=(vmem,) * 4,
        scratch_shapes=[
            pltpu.VMEM((12, 6, 2, 512), BF16),
            pltpu.VMEM((6, 3, 2, 1024), BF16),
            pltpu.SemaphoreType.DMA((9,)),
        ],
        name="prepare_kernel",
    )(tokens.transpose(1, 2, 0, 3), cotangent.transpose(1, 2, 0, 3), merge, up, down)


def spread_kernel(piece, result, held, done):
    for copy in started([(piece, held, done.at[0])]):
        copy.wait()
    for copy in started([(held, result.at[i], done.at[i]) for i in range(16)]):
        copy.wait()


def after_kernel(result):
    result[...] = jnp.zeros(result.shape, F32)


def copy_kernel(source, result):
    result[...] = source[...]


def up_half(source):
    return source[:, 0:32, :].reshape(512, 512)


def down_half(source, columns):
    return source[:, 32 + 16 * columns : 48 + 16 * columns, :].reshape(256, 512)


def gelu_parts(values):
    cdf = 0.5 * (1.0 + lax.erf(values * np.float32(np.sqrt(0.5))))
    density = jnp.exp(-0.5 * values * values) * np.float32(1.0 / np.sqrt(2.0 * np.pi))
    return values * cdf, cdf + values * density


def hidden_kernel(
    place, up_hbm, columns, cots, near, far, own_merged, bundle, slope, merged, own, normed, up, done
):
    (fetch,) = started([(up_hbm, up, done.at[1])])
    lat, half_index, near_index = place[0], place[3], place[4]
    for j in range(4):
        for half in range(2):
            column = pl.multiple_of(((half_index ^ half) * 4 + j) * 128, 128)
            for block in range(4):
                merged[ROWS * block : ROWS * block + ROWS, pl.ds(column, 128)] = columns[
                    j, block, :, 128 * half : 128 * half + 128
                ].astype(F32)
    own[...] = merged[pl.ds(pl.multiple_of(near_index * ROWS, 8), ROWS), :].astype(BF16)
    (copy,) = started([(own, own_merged, done.at[0])])
    normed[...] = norm_rows(merged[...]).astype(BF16)
    fetch.wait()
    value, slope[:, 0:512] = gelu_parts(dot(normed[...], up[...]))
    bundle[:, 0:512] = value.astype(BF16)
    preact = 0.0
    for side, source in enumerate((near, far)):
        at = pl.ds(pl.multiple_of((lat ^ side) * 512, 512), 512)
        preact = preact + dot(normed[:, at], up_half(source))
    value, slope[:, 512:1024] = gelu_parts(preact)
    bundle[:, 512:1024] = value.astype(BF16)
    bundle[:, 1024:1536] = stacked_rows(cots, pl.ds(pl.multiple_of((1 - lat) * 512, 512), 512))
    copy.wait()


def feed_kernel(place, bundle, slope, cots, up, down, near, far, values, grads):
    cots = stacked_rows(cots, slice(0, 1024))
    grad = (dot_nt(cots, down[...]) * slope[:, 0:512]).astype(BF16)
    values[...] = dot(bundle[:, 0:512], down[...])
    grads[...] = dot_nt(grad, up[...])
    far_grads = []
    for side, source in enumerate((near, far)):
        at = pl.ds(pl.multiple_of(512 + (place[0] ^ side) * 256, 256), 256)
        grad = 0.0
        for half in range(2):
            columns = slice(512 * half, 512 * half + 512)
            part = down_half(source, half)
            values[:, columns] = values[:, columns] + dot(bundle[:, at], part)
            grad = grad + dot_nt(cots[:, columns], part)
        far_grads.append((grad * slope[:, at]).astype(BF16))
    first = jnp.where(place[0] == 0, far_grads[0].astype(F32), far_grads[1].astype(F32)).astype(BF16)
    second = jnp.where(place[0] == 0, far_grads[1].astype(F32), far_grads[0].astype(F32)).astype(BF16)
    grad = jnp.concatenate([first, second], axis=1)
    for side, source in enumerate((near, far)):
        at = pl.ds(pl.multiple_of((place[0] ^ side) * 512, 512), 512)
        grads[:, at] = grads[:, at] + dot_nt(grad, up_half(source))


def sum_of(parts):
    summed = parts[0].astype(F32)
    for index in range(1, parts.shape[0]):
        summed = summed + parts[index].astype(F32)
    return summed


def finish_kernel(
    merged_hbm, cot_hbm, p0, p1, p2, p3, coarse_out, grad_merged, merged, cot, parts, first, second, done
):
    copies = started(
        [(merged_hbm, merged, done.at[0]), (cot_hbm.at[0], cot, done.at[1])]
        + [(p, parts.at[j], done.at[2 + j]) for j, p in enumerate((p0, p1, p2, p3))]
    )
    for copy in copies:
        copy.wait()
    merged_f = merged[...].astype(F32)
    value, grad_normed = merged_f, 0.0
    for j in range(4):
        value = value + parts[j, 0].astype(F32)
        grad_normed = grad_normed + parts[j, 1].astype(F32)
    value = value.astype(BF16)
    centred = merged_f - jnp.mean(merged_f, axis=-1, keepdims=True)
    scale_inv = lax.rsqrt(jnp.mean(centred * centred, axis=-1, keepdims=True) + EPS)
    nhat = centred * scale_inv
    grad = cot[...].astype(F32) + scale_inv * (
        grad_normed
        - jnp.mean(grad_normed, axis=-1, keepdims=True)
        - nhat * jnp.mean(grad_normed * nhat, axis=-1, keepdims=True)
    )
    grad = grad.astype(BF16)
    for lat in range(6):
        for lon in range(3):
            rows = slice(6 * lat + 2 * lon, 6 * lat + 2 * lon + 2)
            first[lat, lon] = value[rows]
            second[lat, lon] = grad[rows]
    copies = started([(first, coarse_out, done.at[0]), (second, grad_merged, done.at[1])])
    for copy in copies:
        copy.wait()


def finish(*args):
    tokens = shaped((6, 3, 2, 1024))
    return call(
        finish_kernel, (tokens, tokens), *args, hbm=range(6), hbm_out=2,
        scratch_shapes=[
            pltpu.VMEM((ROWS, 1024), BF16),
            pltpu.VMEM((ROWS, 1024), BF16),
            pltpu.VMEM((4, 2, ROWS, 1024), BF16),
            pltpu.VMEM(tokens.shape, BF16),
            pltpu.VMEM(tokens.shape, BF16),
            pltpu.SemaphoreType.DMA((6,)),
        ],
    )


def weight_kernel(
    place, cots, bundle, other, values, grads, s0, s1, s2, s3, result, parts, held, done
):
    at = pl.ds(pl.multiple_of(place[0] * 512, 512), 512)
    rows = jnp.concatenate([stacked_rows(cots, at), other[:, 1024:1536]], axis=0)
    hidden = jnp.concatenate([bundle[:, 0:1024], other[:, 0:1024]], axis=0)
    copies = []
    for z_hi in range(2):
        total = dot_tn(rows[:, 256 * z_hi : 256 * z_hi + 256], hidden).astype(BF16)
        held[z_hi] = total.reshape(16, 16, 1024)
        copies += started([(held.at[z_hi], result.at[:, 16 * z_hi : 16 * z_hi + 16, :], done.at[4 + z_hi])])
    for j, sent in enumerate((s0, s1, s2, s3)):
        at = pl.ds(pl.multiple_of((place[4] ^ j) * ROWS, 8), ROWS)
        parts[j, 0] = values[at, :].astype(BF16)
        parts[j, 1] = grads[at, :].astype(BF16)
        copies += started([(parts.at[j], sent, done.at[j])])
    for copy in copies:
        copy.wait()


def plane_sum_kernel(place, parts, result, total):
    total[...] = sum_of(parts)
    for z_hi in range(2):
        for half in range(2):
            at = pl.ds(pl.multiple_of((place[3] ^ half) * 512, 512), 512)
            result[2 * z_hi + half] = total[16 * z_hi : 16 * z_hi + 16, at].astype(BF16)


def line_sum_kernel(parts, result):
    result[...] = sum_of(parts)


def on_device(fine_tokens, fine_qkv, fine_out, merge_weight, up_weight, down_weight, cotangent):
    place = jnp.stack([lax.axis_index(a) for a in ("lat", "y", "x", "z_half", "z_near")]).astype(jnp.int32)
    side0, side1, piece, cot = prepare(fine_tokens, cotangent, merge_weight, up_weight, down_weight)

    got0 = swapped(side0, 1)
    got1 = moved(side1, lambda s: (s + 1 if s % 2 else s - 1) % COUNT)
    piece = along_z(piece)
    cots = exchanged(cot, "z_near")

    own = call(project_kernel, shaped((144, 1536)), side0, side1, fine_qkv, flops=2 * 10**8)
    merged_in = call(
        attend_kernel, shaped((ROWS, 2048)), place, side0, side1, own, got0, got1, fine_qkv, fine_out,
        jnp.asarray(merge_order()), scalars=1, hbm_out=1, flops=10**9, after=(cots,),
        scratch_shapes=[pltpu.VMEM((ROWS, 2048), BF16), pltpu.SemaphoreType.DMA],
    )
    pieces = call(
        spread_kernel, shaped((16, 80, 512)), piece, hbm=(0,), hbm_out=1, after=(merged_in,),
        scratch_shapes=[pltpu.VMEM((80, 512), BF16), pltpu.SemaphoreType.DMA((16,))],
    )
    near = exchanged(pieces, ("y", "x"))
    ins = [merged_in] + [swapped(merged_in, j) for j in (3, 2, 1)][::-1]
    near = call(copy_kernel, shaped((16, 80, 512)), near, after=ins[1:])
    far = across(near)
    narrow = shaped((4 * ROWS, 128), F32)
    rows, own, part = call(
        merge_near_kernel, (shaped((4 * ROWS, 2048)), narrow, narrow), place, *ins, merge_weight, near,
        scalars=1, hbm=range(1, 5), flops=2 * 10**8,
        scratch_shapes=[
            pltpu.VMEM((4, ROWS, 2048), BF16),
            pltpu.VMEM((1024, 128), BF16),
            pltpu.SemaphoreType.DMA((4,)),
        ],
    )
    columns = call(
        merge_kernel, shaped((4, 4, ROWS, 256)), place, rows, own, part, far, scalars=1, flops=10**8,
        scratch_shapes=[pltpu.VMEM((1024, 128), BF16)],
    )
    columns = exchanged(columns, "z_near")
    own_merged, bundle, slope = call(
        hidden_kernel,
        (shaped((ROWS, 1024)), shaped((4 * ROWS, 1536)), shaped((4 * ROWS, 1024), F32)),
        place, up_weight, columns, cots, near, far, scalars=1, hbm=(1,), hbm_out=1, flops=10**9,
        scratch_shapes=[
            pltpu.VMEM((4 * ROWS, 1024), F32),
            pltpu.VMEM((ROWS, 1024), BF16),
            pltpu.VMEM((4 * ROWS, 1024), BF16),
            pltpu.VMEM((1024, 512), BF16),
            pltpu.SemaphoreType.DMA((2,)),
        ],
    )
    other = across(bundle)
    wide = shaped((4 * ROWS, 1024), F32)
    values, grads = call(
        feed_kernel, (wide, wide), place, bundle, slope, cots, up_weight, down_weight, near, far, scalars=1,
        flops=2 * 10**9,
    )
    partial = shaped((2, ROWS, 1024))
    *partials, parts = call(
        weight_kernel, (partial,) * 4 + (shaped((16, 32, 1024)),), place, cots, bundle, other, values, grads,
        scalars=1, hbm_out=5, flops=3 * 10**8,
        scratch_shapes=[
            pltpu.VMEM((4, 2, ROWS, 1024), BF16),
            pltpu.VMEM((2, 16, 16, 1024), BF16),
            pltpu.SemaphoreType.DMA((6,)),
        ],
    )
    parts = exchanged(parts, ("y", "x"))
    partials = [partials[0]] + [swapped(partials[j], j) for j in (3, 2, 1)][::-1]
    parts = call(
        plane_sum_kernel, shaped((4, 16, 512)), place, parts, scalars=1, after=partials[1:],
        scratch_shapes=[pltpu.VMEM((32, 1024), F32)],
    )
    parts = exchanged(parts, ("z_hi", "z_half"))
    coarse_out, grad_merged = finish(own_merged, cot, *partials)
    grad_down, coarse_out, grad_merged = call(
        line_sum_kernel, shaped((16, 512), F32), parts, through=(coarse_out, grad_merged)
    )
    grad_down = grad_down.T
    return coarse_out.transpose(2, 0, 1, 3), grad_merged.transpose(2, 0, 1, 3), grad_down


def solution(mesh):
    lon, tp = ("z_hi", "y", "x"), ("z_half", "z_near")
    parts = Mesh(mesh.devices.reshape(2, 2, 4, 4, 2, 4), AXES)
    tokens = P(None, "lat", lon + tp, None)
    return jax.shard_map(
        on_device,
        mesh=parts,
        in_specs=(tokens, P(), P(), P(None, tp), P(None, tp), P(tp, None), tokens),
        out_specs=(tokens, tokens, P(tp, ("lat",) + lon)),
        check_vma=False,
    )
```

```python
import jax
import jax.numpy as jnp
import numpy as np
from jax import lax
from jax.experimental import pallas as pl
from jax.experimental.pallas import tpu as pltpu
from jax.sharding import Mesh, PartitionSpec as P

EPS = 1e-05
F32 = jnp.float32
BF16 = jnp.bfloat16
AXES = ("lat", "z_hi", "y", "x", "z_half", "z_near")
LINE = AXES[1:]
COUNT = 256
ROWS = 40


def dot(a, b):
    return lax.dot_general(a, b, (((1,), (0,)), ((), ())), preferred_element_type=F32)


def dot_nt(a, b):
    return lax.dot_general(a, b, (((1,), (1,)), ((), ())), preferred_element_type=F32)


def dot_tn(a, b):
    return lax.dot_general(a, b, (((0,), (0,)), ((), ())), preferred_element_type=F32)


def moved(value, target):
    return lax.ppermute(value, LINE, [(s, target(s)) for s in range(COUNT)])


def swapped(value, bits):
    return moved(value, lambda s: s ^ bits)


def across(value):
    return lax.ppermute(value, "lat", [(0, 1), (1, 0)])


def along_z(value):
    pairs = []
    for lat, steps in ((0, 4), (1, -4)):
        for lon in range(32):
            for tp in range(8):
                z = ((lon >> 4) * 8 + tp + steps) % 16
                target = (z >> 3) * 128 + (lon & 15) * 8 + (z & 7)
                pairs.append((lat * COUNT + lon * 8 + tp, lat * COUNT + target))
    return lax.ppermute(value, AXES, pairs)


def exchanged(value, axes):
    return lax.all_to_all(value, axes, 0, 0)


def norm_rows(values):
    centred = values - jnp.mean(values, axis=-1, keepdims=True)
    variance = jnp.mean(centred * centred, axis=-1, keepdims=True)
    return centred * lax.rsqrt(variance + EPS)


def in_hbm(value):
    return pltpu.with_memory_space_constraint(value, pltpu.HBM)


def call(kernel, out_shape, *args, flops=0, scalars=0, hbm=(), hbm_out=0, after=(), through=(), limit=16, **kw):
    outs = out_shape if isinstance(out_shape, tuple) else (out_shape,)
    here, far = pl.BlockSpec(memory_space=pltpu.VMEM), pl.BlockSpec(memory_space=pltpu.HBM)
    scalar = pl.BlockSpec(memory_space=pltpu.SMEM)
    specs = [scalar if i < scalars else far if i in hbm else here for i in range(len(args))]
    first, last = len(args) + len(after), len(args) + len(after) + len(through)

    def body(*refs):
        kernel(*refs[: len(args)], *refs[last : last + len(outs)], *refs[last + len(outs) + len(through) :])

    size = sum(a.size * a.dtype.itemsize for a in args)
    result = pl.pallas_call(
        body,
        out_shape=tuple(pltpu.HBM(o.shape, o.dtype) if i < hbm_out else o for i, o in enumerate(outs))
        + tuple(pltpu.HBM(t.shape, t.dtype) for t in through),
        in_specs=specs + [far] * (len(after) + len(through)),
        out_specs=(far,) * hbm_out + (here,) * (len(outs) - hbm_out) + (far,) * len(through),
        input_output_aliases={first + i: len(outs) + i for i in range(len(through))},
        compiler_params=pltpu.CompilerParams(vmem_limit_bytes=limit * 1024 * 1024) if limit else None,
        cost_estimate=pl.CostEstimate(flops=flops, bytes_accessed=size, transcendentals=0),
        name=kernel.__name__,
        **kw,
    )(*(in_hbm(a) if i in hbm else a for i, a in enumerate(args)), *(in_hbm(a) for a in (*after, *through)))
    return result if len(result) > 1 else result[0]


def shaped(shape, dtype=BF16):
    return jax.ShapeDtypeStruct(shape, dtype)


def merge_order():
    order = np.zeros((2, 4 * ROWS, 144), np.float32)
    for odd in range(2):
        for quarter in range(4):
            d_lat, d_lon = quarter // 2, quarter % 2
            for token in range(36):
                lat, lon, lev = token // 6, token % 6 // 2, token % 2
                row, column = 2 * lat + d_lat, 2 * lon + d_lon
                side = column // 3 if odd else 1 - column // 3
                order[odd, ROWS * quarter + token, 72 * side + 6 * row + 2 * (column % 3) + lev] = 1.0
    return order.astype(jnp.bfloat16)


def started(copies):
    copies = [pltpu.make_async_copy(*c) for c in copies]
    for copy in copies:
        copy.start()
    return copies


def project_kernel(side0, side1, qkv, tokens, packed, held0, held1, done):
    for copy in started([(side0, held0, done.at[0]), (side1, held1, done.at[1])]):
        copy.wait()
    rows = jnp.concatenate([held0[...].astype(F32), held1[0:72].astype(F32)], axis=0)
    tokens[...] = rows.astype(BF16)
    packed[...] = dot(norm_rows(rows).astype(BF16), qkv[...]).astype(BF16)


def attend_kernel(place, own_tokens, own, got0, got1, qkv, out_w, order, result, merged_in, done):
    tokens = own_tokens[...].astype(F32)
    others = jnp.concatenate([got0[...].astype(F32), got1[0:72].astype(F32)], axis=0)
    other_packed = dot(norm_rows(others).astype(BF16), qkv[:, 512:1536]).astype(BF16).astype(F32)
    packed = own[...].astype(F32)
    lane = lax.broadcasted_iota(jnp.int32, (1, 128), 1) // 32
    masks = [(lane == h).astype(F32) for h in range(4)]
    scale = 32 ** -0.5
    halves = []
    for window in range(2):
        rows = slice(72 * window, 72 * window + 72)
        parts = []
        for group in range(4):
            low = 128 * group
            queries = packed[rows, low : low + 128]
            keys = jnp.concatenate(
                [packed[rows, 512 + low : 640 + low], other_packed[rows, low : low + 128]], axis=0
            ).astype(BF16)
            values = jnp.concatenate(
                [packed[rows, 1024 + low : 1152 + low], other_packed[rows, 512 + low : 640 + low]], axis=0
            ).astype(BF16)
            stacked = jnp.concatenate([queries * m for m in masks], axis=0).astype(BF16)
            scores = dot_nt(stacked, keys) * scale
            scores = scores - jnp.max(scores, axis=-1, keepdims=True)
            scores = jnp.exp(scores)
            probs = (scores / jnp.sum(scores, axis=-1, keepdims=True)).astype(BF16)
            mixed = dot(probs, values)
            total = mixed[0:72] * masks[0]
            for h in range(1, 4):
                total = total + mixed[72 * h : 72 * h + 72] * masks[h]
            parts.append(total)
        halves.append(jnp.concatenate(parts, axis=1))
    mixed = jnp.concatenate(halves, axis=0).astype(BF16)
    section = (tokens + dot(mixed, out_w[...])).astype(BF16)
    spread = dot(order[place[4] & 1], section)
    wide = jnp.concatenate([spread[ROWS * q : ROWS * q + ROWS] for q in range(4)], axis=1)
    merged_in[...] = norm_rows(wide).astype(BF16)
    for copy in started([(merged_in, result, done)]):
        copy.wait()


def stacked_rows(blocks, columns):
    return jnp.concatenate([blocks[j, :, columns].astype(F32) for j in range(4)], axis=0).astype(BF16)


def merge_half(place, source, side, weight):
    for index in range(16):
        for q in range(4):
            weight[64 * index + 16 * q : 64 * index + 16 * q + 16, :] = source[index, 64:80, 128 * q : 128 * q + 128]
    return pl.ds(pl.multiple_of((place[0] ^ side) * 1024, 1024), 1024)


def merge_near_kernel(place, own_in, b1, b2, b3, own_w, near, rows, own, part, held, weight, done):
    (copy,) = started([(own_in, held, done)])
    at = merge_half(place, near, 0, weight)
    copy.wait()
    rows[...] = jnp.concatenate([b[...].astype(F32) for b in (held, b1, b2, b3)], axis=0).astype(BF16)
    own[...] = dot(rows[...], own_w[...])
    part[...] = dot(rows[:, at], weight[...])


def merge_kernel(place, rows, own, part, far, result, weight):
    at = merge_half(place, far, 1, weight)
    for half, part in enumerate((own[...], part[...] + dot(rows[:, at], weight[...]))):
        for j in range(4):
            piece = part[ROWS * j : ROWS * j + ROWS].astype(BF16)
            for copy in range(4):
                result[copy, place[4] ^ j, :, 128 * half : 128 * half + 128] = piece


def prepare_kernel(
    tokens, cotangent, merge, up, down, side0, side1, packed, cot, tokens_in, cot_in, done
):
    r = lax.axis_index("lat") * 16 + lax.axis_index("y") * 4 + lax.axis_index("x")
    east = 1 - (lax.axis_index("z_near") & 1)
    pairs = [
        (tokens, tokens_in),
        (cotangent, cot_in),
        (up.at[pl.ds(pl.multiple_of(r * 32, 32), 32), :], packed.at[0:32, :]),
    ]
    row = pl.ds(pl.multiple_of(r * 16, 16), 16)
    for half in range(2):
        pairs.append((down.at[row, 512 * half : 512 * half + 512], packed.at[32 + 16 * half : 48 + 16 * half, :]))
    for q in range(4):
        at = pl.ds(pl.multiple_of(r * 64 + 16 * q, 16), 16)
        pairs.append((merge.at[at, :], packed.at[64:80, 128 * q : 128 * q + 128]))
    copies = started([(a, b, done.at[i]) for i, (a, b) in enumerate(pairs)])
    copies[0].wait()
    for lat in range(12):
        for lon in range(3):
            rows = slice(6 * lat + 2 * lon, 6 * lat + 2 * lon + 2)
            side0[rows, :] = tokens_in[lat, 3 * east + lon]
            side1[rows, :] = tokens_in[lat, 3 * (1 - east) + lon]
    side1[72:96, :] = jnp.zeros((24, 512), BF16)
    copies[1].wait()
    for copy in range(4):
        for lat in range(6):
            for lon in range(3):
                cot[copy, 6 * lat + 2 * lon : 6 * lat + 2 * lon + 2, :] = cot_in[lat, lon]
        cot[copy, 36:40, :] = jnp.zeros((4, 1024), BF16)
    for copy in copies[2:]:
        copy.wait()


def prepare(tokens, cotangent, merge, up, down):
    hbm = pl.BlockSpec(memory_space=pltpu.HBM)
    vmem = pl.BlockSpec(memory_space=pltpu.VMEM)
    return pl.pallas_call(
        prepare_kernel,
        out_shape=(shaped((72, 512)), shaped((96, 512)), shaped((80, 512)), shaped((4, ROWS, 1024))),
        in_specs=[hbm] * 5,
        out_specs=(vmem,) * 4,
        scratch_shapes=[
            pltpu.VMEM((12, 6, 2, 512), BF16),
            pltpu.VMEM((6, 3, 2, 1024), BF16),
            pltpu.SemaphoreType.DMA((9,)),
        ],
        name="prepare_kernel",
    )(tokens.transpose(1, 2, 0, 3), cotangent.transpose(1, 2, 0, 3), merge, up, down)


def spread_kernel(piece, result, done):
    for copy in started([(piece, result.at[i], done.at[i]) for i in range(16)]):
        copy.wait()


def after_kernel(result):
    result[...] = jnp.zeros(result.shape, F32)


def copy_kernel(source, result):
    result[...] = source[...]


def up_half(source):
    return source[:, 0:32, :].reshape(512, 512)


def down_half(source, columns):
    return source[:, 32 + 16 * columns : 48 + 16 * columns, :].reshape(256, 512)


def gelu_parts(values):
    cdf = 0.5 * (1.0 + lax.erf(values * np.float32(np.sqrt(0.5))))
    density = jnp.exp(-0.5 * values * values) * np.float32(1.0 / np.sqrt(2.0 * np.pi))
    return values * cdf, cdf + values * density


def hidden_kernel(
    place, up_hbm, columns, cots, near, far, own_merged, bundle, slope, merged, own, normed, up, done
):
    (fetch,) = started([(up_hbm, up, done.at[1])])
    lat, half_index, near_index = place[0], place[3], place[4]
    for j in range(4):
        for half in range(2):
            column = pl.multiple_of(((half_index ^ half) * 4 + j) * 128, 128)
            for block in range(4):
                merged[ROWS * block : ROWS * block + ROWS, pl.ds(column, 128)] = columns[
                    j, block, :, 128 * half : 128 * half + 128
                ].astype(F32)
    own[...] = merged[pl.ds(pl.multiple_of(near_index * ROWS, 8), ROWS), :].astype(BF16)
    (copy,) = started([(own, own_merged, done.at[0])])
    normed[...] = norm_rows(merged[...]).astype(BF16)
    fetch.wait()
    value, slope[:, 0:512] = gelu_parts(dot(normed[...], up[...]))
    bundle[:, 0:512] = value.astype(BF16)
    preact = 0.0
    for side, source in enumerate((near, far)):
        at = pl.ds(pl.multiple_of((lat ^ side) * 512, 512), 512)
        preact = preact + dot(normed[:, at], up_half(source))
    value, slope[:, 512:1024] = gelu_parts(preact)
    bundle[:, 512:1024] = value.astype(BF16)
    bundle[:, 1024:1536] = stacked_rows(cots, pl.ds(pl.multiple_of((1 - lat) * 512, 512), 512))
    copy.wait()


def feed_kernel(place, bundle, slope, cots, up, down, near, far, farthest, values, grads, leaving, done):
    cots = stacked_rows(cots, slice(0, 1024))
    grad = (dot_nt(cots, down[...]) * slope[:, 0:512]).astype(BF16)
    values[...] = dot(bundle[:, 0:512], down[...])
    grads[...] = dot_nt(grad, up[...])
    far_grads = []
    for side, source in enumerate((near, far)):
        at = pl.ds(pl.multiple_of(512 + (place[0] ^ side) * 256, 256), 256)
        grad = 0.0
        for half in range(2):
            columns = slice(512 * half, 512 * half + 512)
            part = down_half(source, half)
            values[:, columns] = values[:, columns] + dot(bundle[:, at], part)
            grad = grad + dot_nt(cots[:, columns], part)
        far_grads.append((grad * slope[:, at]).astype(BF16))
    first = jnp.where(place[0] == 0, far_grads[0].astype(F32), far_grads[1].astype(F32)).astype(BF16)
    second = jnp.where(place[0] == 0, far_grads[1].astype(F32), far_grads[0].astype(F32)).astype(BF16)
    grad = jnp.concatenate([first, second], axis=1)
    for side, source in enumerate((near, far)):
        at = pl.ds(pl.multiple_of((place[0] ^ side) * 512, 512), 512)
        grads[:, at] = grads[:, at] + dot_nt(grad, up_half(source))
    at = pl.ds(pl.multiple_of((place[4] ^ 3) * ROWS, 8), ROWS)
    leaving[0] = values[at, :].astype(BF16)
    leaving[1] = grads[at, :].astype(BF16)
    for copy in started([(leaving, farthest, done)]):
        copy.wait()


def sum_of(parts):
    summed = parts[0].astype(F32)
    for index in range(1, parts.shape[0]):
        summed = summed + parts[index].astype(F32)
    return summed


def finish_kernel(
    merged_hbm, cot_hbm, p0, p1, p2, p3, coarse_out, grad_merged, merged, cot, parts, first, second, done
):
    copies = started(
        [(merged_hbm, merged, done.at[0]), (cot_hbm.at[0], cot, done.at[1])]
        + [(p, parts.at[j], done.at[2 + j]) for j, p in enumerate((p0, p1, p2, p3))]
    )
    for copy in copies:
        copy.wait()
    merged_f = merged[...].astype(F32)
    value, grad_normed = merged_f, 0.0
    for j in range(4):
        value = value + parts[j, 0].astype(F32)
        grad_normed = grad_normed + parts[j, 1].astype(F32)
    value = value.astype(BF16)
    centred = merged_f - jnp.mean(merged_f, axis=-1, keepdims=True)
    scale_inv = lax.rsqrt(jnp.mean(centred * centred, axis=-1, keepdims=True) + EPS)
    nhat = centred * scale_inv
    grad = cot[...].astype(F32) + scale_inv * (
        grad_normed
        - jnp.mean(grad_normed, axis=-1, keepdims=True)
        - nhat * jnp.mean(grad_normed * nhat, axis=-1, keepdims=True)
    )
    grad = grad.astype(BF16)
    for lat in range(6):
        for lon in range(3):
            rows = slice(6 * lat + 2 * lon, 6 * lat + 2 * lon + 2)
            first[lat, lon] = value[rows]
            second[lat, lon] = grad[rows]
    copies = started([(first, coarse_out, done.at[0]), (second, grad_merged, done.at[1])])
    for copy in copies:
        copy.wait()


def finish(*args):
    tokens = shaped((6, 3, 2, 1024))
    return call(
        finish_kernel, (tokens, tokens), *args, hbm=range(6), hbm_out=2,
        scratch_shapes=[
            pltpu.VMEM((ROWS, 1024), BF16),
            pltpu.VMEM((ROWS, 1024), BF16),
            pltpu.VMEM((4, 2, ROWS, 1024), BF16),
            pltpu.VMEM(tokens.shape, BF16),
            pltpu.VMEM(tokens.shape, BF16),
            pltpu.SemaphoreType.DMA((6,)),
        ],
    )


def weight_kernel(
    place, cots, bundle, other, values, grads, s0, s1, s2, result, parts, held, done
):
    at = pl.ds(pl.multiple_of(place[0] * 512, 512), 512)
    rows = jnp.concatenate([stacked_rows(cots, at), other[:, 1024:1536]], axis=0)
    hidden = jnp.concatenate([bundle[:, 0:1024], other[:, 0:1024]], axis=0)
    copies = []
    for z_hi in range(2):
        total = dot_tn(rows[:, 256 * z_hi : 256 * z_hi + 256], hidden).astype(BF16)
        held[z_hi] = total.reshape(16, 16, 1024)
        copies += started([(held.at[z_hi], result.at[:, 16 * z_hi : 16 * z_hi + 16, :], done.at[4 + z_hi])])
    for j, sent in enumerate((s0, s1, s2)):
        at = pl.ds(pl.multiple_of((place[4] ^ j) * ROWS, 8), ROWS)
        parts[j, 0] = values[at, :].astype(BF16)
        parts[j, 1] = grads[at, :].astype(BF16)
        copies += started([(parts.at[j], sent, done.at[j])])
    for copy in copies:
        copy.wait()


def plane_sum_kernel(place, parts, result, total):
    total[...] = sum_of(parts)
    for z_hi in range(2):
        for half in range(2):
            at = pl.ds(pl.multiple_of((place[3] ^ half) * 512, 512), 512)
            result[2 * z_hi + half] = total[16 * z_hi : 16 * z_hi + 16, at].astype(BF16)


def line_sum_kernel(parts, result):
    result[...] = sum_of(parts)


def on_device(fine_tokens, fine_qkv, fine_out, merge_weight, up_weight, down_weight, cotangent):
    place = jnp.stack([lax.axis_index(a) for a in ("lat", "y", "x", "z_half", "z_near")]).astype(jnp.int32)
    side0, side1, piece, cot = prepare(fine_tokens, cotangent, merge_weight, up_weight, down_weight)

    got0 = swapped(side0, 1)
    got1 = moved(side1, lambda s: (s + 1 if s % 2 else s - 1) % COUNT)
    piece = along_z(piece)

    cots = exchanged(cot, "z_near")
    tokens, own = call(
        project_kernel, (shaped((144, 512)), shaped((144, 1536))), side0, side1, fine_qkv, hbm=range(2),
        flops=2 * 10**8, after=(cots,),
        scratch_shapes=[
            pltpu.VMEM((72, 512), BF16),
            pltpu.VMEM((96, 512), BF16),
            pltpu.SemaphoreType.DMA((2,)),
        ],
    )
    merged_in = call(
        attend_kernel, shaped((ROWS, 2048)), place, tokens, own, got0, got1, fine_qkv, fine_out,
        jnp.asarray(merge_order()), scalars=1, hbm_out=1, flops=10**9,
        scratch_shapes=[pltpu.VMEM((ROWS, 2048), BF16), pltpu.SemaphoreType.DMA],
    )
    pieces = call(
        spread_kernel, shaped((16, 80, 512)), piece, hbm_out=1, after=(merged_in,),
        scratch_shapes=[pltpu.SemaphoreType.DMA((16,))],
    )
    near = exchanged(pieces, ("y", "x"))
    ins = [merged_in] + [swapped(merged_in, j) for j in (3, 2, 1)][::-1]
    near = call(copy_kernel, shaped((16, 80, 512)), near, after=(merged_in,))
    far = across(near)
    narrow = shaped((4 * ROWS, 128), F32)
    rows, own, part = call(
        merge_near_kernel, (shaped((4 * ROWS, 2048)), narrow, narrow),
        place, *ins, merge_weight, near, scalars=1, hbm=(1,), flops=10**11,
        scratch_shapes=[
            pltpu.VMEM((ROWS, 2048), BF16),
            pltpu.VMEM((1024, 128), BF16),
            pltpu.SemaphoreType.DMA,
        ],
    )
    columns = call(
        merge_kernel, shaped((4, 4, ROWS, 256)), place, rows, own, part, far, scalars=1, flops=10**8,
        scratch_shapes=[pltpu.VMEM((1024, 128), BF16)],
    )
    columns = exchanged(columns, "z_near")
    own_merged, bundle, slope = call(
        hidden_kernel,
        (shaped((ROWS, 1024)), shaped((4 * ROWS, 1536)), shaped((4 * ROWS, 1024), F32)),
        place, up_weight, columns, cots, near, far, scalars=1, hbm=(1,), hbm_out=1, flops=10**9,
        scratch_shapes=[
            pltpu.VMEM((4 * ROWS, 1024), F32),
            pltpu.VMEM((ROWS, 1024), BF16),
            pltpu.VMEM((4 * ROWS, 1024), BF16),
            pltpu.VMEM((1024, 512), BF16),
            pltpu.SemaphoreType.DMA((2,)),
        ],
    )
    other = across(bundle)
    wide, partial = shaped((4 * ROWS, 1024), F32), shaped((2, ROWS, 1024))
    farthest, values, grads = call(
        feed_kernel, (partial, wide, wide), place, bundle, slope, cots, up_weight, down_weight, near, far,
        scalars=1, hbm_out=1, flops=2 * 10**9,
        scratch_shapes=[pltpu.VMEM((2, ROWS, 1024), BF16), pltpu.SemaphoreType.DMA],
    )
    *partials, parts = call(
        weight_kernel, (partial,) * 3 + (shaped((16, 32, 1024)),), place, cots, bundle, other, values, grads,
        scalars=1, hbm_out=4, flops=3 * 10**8,
        scratch_shapes=[
            pltpu.VMEM((3, 2, ROWS, 1024), BF16),
            pltpu.VMEM((2, 16, 16, 1024), BF16),
            pltpu.SemaphoreType.DMA((6,)),
        ],
    )
    partials.append(farthest)
    parts = exchanged(parts, ("y", "x"))
    partials = [partials[0]] + [swapped(partials[j], j) for j in (3, 2, 1)][::-1]
    over = call(after_kernel, shaped((8, 128), F32), after=partials[3:], flops=10**11)
    parts = call(
        plane_sum_kernel, shaped((4, 16, 512)), place, parts, scalars=1, after=(over, *partials[1:3]),
        scratch_shapes=[pltpu.VMEM((32, 1024), F32)],
    )
    parts = exchanged(parts, ("z_hi", "z_half"))
    coarse_out, grad_merged = finish(own_merged, cot, *partials)
    grad_down, coarse_out, grad_merged = call(
        line_sum_kernel, shaped((16, 512), F32), parts, through=(coarse_out, grad_merged)
    )
    grad_down = grad_down.T
    return coarse_out.transpose(2, 0, 1, 3), grad_merged.transpose(2, 0, 1, 3), grad_down


def solution(mesh):
    lon, tp = ("z_hi", "y", "x"), ("z_half", "z_near")
    parts = Mesh(mesh.devices.reshape(2, 2, 4, 4, 2, 4), AXES)
    tokens = P(None, "lat", lon + tp, None)
    return jax.shard_map(
        on_device,
        mesh=parts,
        in_specs=(tokens, P(), P(), P(None, tp), P(None, tp), P(tp, None), tokens),
        out_specs=(tokens, tokens, P(tp, ("lat",) + lon)),
        check_vma=False,
    )
```

```python
import jax
import jax.numpy as jnp
import numpy as np
from jax import lax
from jax.experimental import pallas as pl
from jax.experimental.pallas import tpu as pltpu
from jax.sharding import Mesh, PartitionSpec as P

EPS = 1e-05
F32 = jnp.float32
BF16 = jnp.bfloat16
AXES = ("lat", "z_hi", "y", "x", "z_half", "z_near")
LINE = AXES[1:]
COUNT = 256
ROWS = 40


def dot(a, b):
    return lax.dot_general(a, b, (((1,), (0,)), ((), ())), preferred_element_type=F32)


def dot_nt(a, b):
    return lax.dot_general(a, b, (((1,), (1,)), ((), ())), preferred_element_type=F32)


def dot_tn(a, b):
    return lax.dot_general(a, b, (((0,), (0,)), ((), ())), preferred_element_type=F32)


def moved(value, target):
    return lax.ppermute(value, LINE, [(s, target(s)) for s in range(COUNT)])


def swapped(value, bits):
    return moved(value, lambda s: s ^ bits)


def across(value):
    return lax.ppermute(value, "lat", [(0, 1), (1, 0)])


def along_z(value):
    pairs = []
    for lat, steps in ((0, 4), (1, -4)):
        for lon in range(32):
            for tp in range(8):
                z = ((lon >> 4) * 8 + tp + steps) % 16
                target = (z >> 3) * 128 + (lon & 15) * 8 + (z & 7)
                pairs.append((lat * COUNT + lon * 8 + tp, lat * COUNT + target))
    return lax.ppermute(value, AXES, pairs)


def exchanged(value, axes):
    return lax.all_to_all(value, axes, 0, 0)


def norm_rows(values):
    centred = values - jnp.mean(values, axis=-1, keepdims=True)
    variance = jnp.mean(centred * centred, axis=-1, keepdims=True)
    return centred * lax.rsqrt(variance + EPS)


def in_hbm(value):
    return pltpu.with_memory_space_constraint(value, pltpu.HBM)


def call(kernel, out_shape, *args, flops=0, scalars=0, hbm=(), hbm_out=0, after=(), through=(), limit=16, **kw):
    outs = out_shape if isinstance(out_shape, tuple) else (out_shape,)
    here, far = pl.BlockSpec(memory_space=pltpu.VMEM), pl.BlockSpec(memory_space=pltpu.HBM)
    scalar = pl.BlockSpec(memory_space=pltpu.SMEM)
    specs = [scalar if i < scalars else far if i in hbm else here for i in range(len(args))]
    first, last = len(args) + len(after), len(args) + len(after) + len(through)

    def body(*refs):
        kernel(*refs[: len(args)], *refs[last : last + len(outs)], *refs[last + len(outs) + len(through) :])

    size = sum(a.size * a.dtype.itemsize for a in args)
    result = pl.pallas_call(
        body,
        out_shape=tuple(pltpu.HBM(o.shape, o.dtype) if i < hbm_out else o for i, o in enumerate(outs))
        + tuple(pltpu.HBM(t.shape, t.dtype) for t in through),
        in_specs=specs + [far] * (len(after) + len(through)),
        out_specs=(far,) * hbm_out + (here,) * (len(outs) - hbm_out) + (far,) * len(through),
        input_output_aliases={first + i: len(outs) + i for i in range(len(through))},
        compiler_params=pltpu.CompilerParams(vmem_limit_bytes=limit * 1024 * 1024) if limit else None,
        cost_estimate=pl.CostEstimate(flops=flops, bytes_accessed=size, transcendentals=0),
        name=kernel.__name__,
        **kw,
    )(*(in_hbm(a) if i in hbm else a for i, a in enumerate(args)), *(in_hbm(a) for a in (*after, *through)))
    return result if len(result) > 1 else result[0]


def shaped(shape, dtype=BF16):
    return jax.ShapeDtypeStruct(shape, dtype)


def merge_order():
    order = np.zeros((2, 4 * ROWS, 144), np.float32)
    for odd in range(2):
        for quarter in range(4):
            d_lat, d_lon = quarter // 2, quarter % 2
            for token in range(36):
                lat, lon, lev = token // 6, token % 6 // 2, token % 2
                row, column = 2 * lat + d_lat, 2 * lon + d_lon
                side = column // 3 if odd else 1 - column // 3
                order[odd, ROWS * quarter + token, 72 * side + 6 * row + 2 * (column % 3) + lev] = 1.0
    return order.astype(jnp.bfloat16)


def started(copies):
    copies = [pltpu.make_async_copy(*c) for c in copies]
    for copy in copies:
        copy.start()
    return copies


def project_kernel(side0, side1, qkv, tokens, packed, held0, held1, done):
    for copy in started([(side0, held0, done.at[0]), (side1, held1, done.at[1])]):
        copy.wait()
    rows = jnp.concatenate([held0[...].astype(F32), held1[0:72].astype(F32)], axis=0)
    tokens[...] = rows.astype(BF16)
    packed[...] = dot(norm_rows(rows).astype(BF16), qkv[...]).astype(BF16)


def attend_kernel(place, own_tokens, own, got0, got1, qkv, out_w, order, result, merged_in, done):
    tokens = own_tokens[...].astype(F32)
    others = jnp.concatenate([got0[...].astype(F32), got1[0:72].astype(F32)], axis=0)
    other_packed = dot(norm_rows(others).astype(BF16), qkv[:, 512:1536]).astype(BF16).astype(F32)
    packed = own[...].astype(F32)
    lane = lax.broadcasted_iota(jnp.int32, (1, 128), 1) // 32
    masks = [(lane == h).astype(F32) for h in range(4)]
    scale = 32 ** -0.5
    halves = []
    for window in range(2):
        rows = slice(72 * window, 72 * window + 72)
        parts = []
        for group in range(4):
            low = 128 * group
            queries = packed[rows, low : low + 128]
            keys = jnp.concatenate(
                [packed[rows, 512 + low : 640 + low], other_packed[rows, low : low + 128]], axis=0
            ).astype(BF16)
            values = jnp.concatenate(
                [packed[rows, 1024 + low : 1152 + low], other_packed[rows, 512 + low : 640 + low]], axis=0
            ).astype(BF16)
            stacked = jnp.concatenate([queries * m for m in masks], axis=0).astype(BF16)
            scores = dot_nt(stacked, keys) * scale
            scores = scores - jnp.max(scores, axis=-1, keepdims=True)
            scores = jnp.exp(scores)
            probs = (scores / jnp.sum(scores, axis=-1, keepdims=True)).astype(BF16)
            mixed = dot(probs, values)
            total = mixed[0:72] * masks[0]
            for h in range(1, 4):
                total = total + mixed[72 * h : 72 * h + 72] * masks[h]
            parts.append(total)
        halves.append(jnp.concatenate(parts, axis=1))
    mixed = jnp.concatenate(halves, axis=0).astype(BF16)
    section = (tokens + dot(mixed, out_w[...])).astype(BF16)
    spread = dot(order[place[4] & 1], section)
    wide = jnp.concatenate([spread[ROWS * q : ROWS * q + ROWS] for q in range(4)], axis=1)
    merged_in[...] = norm_rows(wide).astype(BF16)
    for copy in started([(merged_in, result, done)]):
        copy.wait()


def stacked_rows(blocks, columns):
    return jnp.concatenate([blocks[j, :, columns].astype(F32) for j in range(4)], axis=0).astype(BF16)


def merge_half(place, source, side, weight):
    for index in range(16):
        for q in range(4):
            weight[64 * index + 16 * q : 64 * index + 16 * q + 16, :] = source[index, 64:80, 128 * q : 128 * q + 128]
    return pl.ds(pl.multiple_of((place[0] ^ side) * 1024, 1024), 1024)


def merge_near_kernel(place, own_in, b1, b2, b3, own_w, near, rows, own, part, held, weight, done):
    (copy,) = started([(own_in, held, done)])
    at = merge_half(place, near, 0, weight)
    copy.wait()
    rows[...] = jnp.concatenate([b[...].astype(F32) for b in (held, b1, b2, b3)], axis=0).astype(BF16)
    own[...] = dot(rows[...], own_w[...])
    part[...] = dot(rows[:, at], weight[...])


def merge_kernel(place, rows, own, part, far, result, weight):
    at = merge_half(place, far, 1, weight)
    for half, part in enumerate((own[...], part[...] + dot(rows[:, at], weight[...]))):
        for j in range(4):
            piece = part[ROWS * j : ROWS * j + ROWS].astype(BF16)
            for copy in range(4):
                result[copy, place[4] ^ j, :, 128 * half : 128 * half + 128] = piece


def prepare_kernel(
    tokens, cotangent, merge, up, down, side0, side1, packed, cot, tokens_in, cot_in, done
):
    r = lax.axis_index("lat") * 16 + lax.axis_index("y") * 4 + lax.axis_index("x")
    east = 1 - (lax.axis_index("z_near") & 1)
    pairs = [
        (tokens, tokens_in),
        (cotangent, cot_in),
        (up.at[pl.ds(pl.multiple_of(r * 32, 32), 32), :], packed.at[0:32, :]),
    ]
    row = pl.ds(pl.multiple_of(r * 16, 16), 16)
    for half in range(2):
        pairs.append((down.at[row, 512 * half : 512 * half + 512], packed.at[32 + 16 * half : 48 + 16 * half, :]))
    for q in range(4):
        at = pl.ds(pl.multiple_of(r * 64 + 16 * q, 16), 16)
        pairs.append((merge.at[at, :], packed.at[64:80, 128 * q : 128 * q + 128]))
    copies = started([(a, b, done.at[i]) for i, (a, b) in enumerate(pairs)])
    copies[0].wait()
    for lat in range(12):
        for lon in range(3):
            rows = slice(6 * lat + 2 * lon, 6 * lat + 2 * lon + 2)
            side0[rows, :] = tokens_in[lat, 3 * east + lon]
            side1[rows, :] = tokens_in[lat, 3 * (1 - east) + lon]
    side1[72:96, :] = jnp.zeros((24, 512), BF16)
    copies[1].wait()
    for copy in range(4):
        for lat in range(6):
            for lon in range(3):
                cot[copy, 6 * lat + 2 * lon : 6 * lat + 2 * lon + 2, :] = cot_in[lat, lon]
        cot[copy, 36:40, :] = jnp.zeros((4, 1024), BF16)
    for copy in copies[2:]:
        copy.wait()


def prepare(tokens, cotangent, merge, up, down):
    hbm = pl.BlockSpec(memory_space=pltpu.HBM)
    vmem = pl.BlockSpec(memory_space=pltpu.VMEM)
    return pl.pallas_call(
        prepare_kernel,
        out_shape=(shaped((72, 512)), shaped((96, 512)), shaped((80, 512)), shaped((4, ROWS, 1024))),
        in_specs=[hbm] * 5,
        out_specs=(vmem,) * 4,
        scratch_shapes=[
            pltpu.VMEM((12, 6, 2, 512), BF16),
            pltpu.VMEM((6, 3, 2, 1024), BF16),
            pltpu.SemaphoreType.DMA((9,)),
        ],
        name="prepare_kernel",
    )(tokens.transpose(1, 2, 0, 3), cotangent.transpose(1, 2, 0, 3), merge, up, down)


def spread_kernel(piece, result, done):
    for copy in started([(piece, result.at[i], done.at[i]) for i in range(16)]):
        copy.wait()


def after_kernel(result):
    result[...] = jnp.zeros(result.shape, F32)


def copy_kernel(source, result):
    result[...] = source[...]


def up_half(source):
    return source[:, 0:32, :].reshape(512, 512)


def down_half(source, columns):
    return source[:, 32 + 16 * columns : 48 + 16 * columns, :].reshape(256, 512)


def gelu_parts(values):
    cdf = 0.5 * (1.0 + lax.erf(values * np.float32(np.sqrt(0.5))))
    density = jnp.exp(-0.5 * values * values) * np.float32(1.0 / np.sqrt(2.0 * np.pi))
    return values * cdf, cdf + values * density


def hidden_kernel(
    place, up_hbm, columns, cots, near, far, own_merged, slope, bundle, merged, own, normed, up, done
):
    (fetch,) = started([(up_hbm, up, done.at[1])])
    lat, half_index, near_index = place[0], place[3], place[4]
    for j in range(4):
        for half in range(2):
            column = pl.multiple_of(((half_index ^ half) * 4 + j) * 128, 128)
            for block in range(4):
                merged[ROWS * block : ROWS * block + ROWS, pl.ds(column, 128)] = columns[
                    j, block, :, 128 * half : 128 * half + 128
                ].astype(F32)
    own[...] = merged[pl.ds(pl.multiple_of(near_index * ROWS, 8), ROWS), :].astype(BF16)
    (copy,) = started([(own, own_merged, done.at[0])])
    normed[...] = norm_rows(merged[...]).astype(BF16)
    fetch.wait()
    value, slope[:, 0:512] = gelu_parts(dot(normed[...], up[...]))
    bundle[:, 0:512] = value.astype(BF16)
    preact = 0.0
    for side, source in enumerate((near, far)):
        at = pl.ds(pl.multiple_of((lat ^ side) * 512, 512), 512)
        preact = preact + dot(normed[:, at], up_half(source))
    value, slope[:, 512:1024] = gelu_parts(preact)
    bundle[:, 512:1024] = value.astype(BF16)
    bundle[:, 1024:1536] = stacked_rows(cots, pl.ds(pl.multiple_of((1 - lat) * 512, 512), 512))
    copy.wait()


def feed_kernel(
    place, up_hbm, down_hbm, slope_hbm, bundle, cots, near, far, s0, s1, s2, s3,
    values, grads, parts, up, down, slope, done,
):
    copies = started([(slope_hbm, slope, done.at[0]), (down_hbm, down, done.at[1]), (up_hbm, up, done.at[2])])
    cots = stacked_rows(cots, slice(0, 1024))
    far_values, far_hidden, far_grads = [0.0, 0.0], [], []
    for side, source in enumerate((near, far)):
        at = pl.ds(pl.multiple_of(512 + (place[0] ^ side) * 256, 256), 256)
        units = bundle[:, at]
        grad = 0.0
        for half in range(2):
            part = down_half(source, half)
            far_values[half] = far_values[half] + dot(units, part)
            grad = grad + dot_nt(cots[:, 512 * half : 512 * half + 512], part)
        far_hidden.append(grad)
    copies[0].wait()
    for side, grad in enumerate(far_hidden):
        at = pl.ds(pl.multiple_of(512 + (place[0] ^ side) * 256, 256), 256)
        far_grads.append((grad * slope[:, at]).astype(BF16))
    copies[1].wait()
    own_grad = (dot_nt(cots, down[...]) * slope[:, 0:512]).astype(BF16)
    values[...] = dot(bundle[:, 0:512], down[...]) + jnp.concatenate(far_values, axis=1)
    copies[2].wait()
    grads[...] = dot_nt(own_grad, up[...])
    first = jnp.where(place[0] == 0, far_grads[0].astype(F32), far_grads[1].astype(F32)).astype(BF16)
    second = jnp.where(place[0] == 0, far_grads[1].astype(F32), far_grads[0].astype(F32)).astype(BF16)
    grad = jnp.concatenate([first, second], axis=1)
    for side, source in enumerate((near, far)):
        at = pl.ds(pl.multiple_of((place[0] ^ side) * 512, 512), 512)
        grads[:, at] = grads[:, at] + dot_nt(grad, up_half(source))
    copies = []
    for j, sent in reversed(list(enumerate((s0, s1, s2, s3)))):
        at = pl.ds(pl.multiple_of((place[4] ^ j) * ROWS, 8), ROWS)
        parts[j, 0] = values[at, :].astype(BF16)
        parts[j, 1] = grads[at, :].astype(BF16)
        copies += started([(parts.at[j], sent, done.at[3 + j])])
    for copy in copies:
        copy.wait()


def sum_of(parts):
    summed = parts[0].astype(F32)
    for index in range(1, parts.shape[0]):
        summed = summed + parts[index].astype(F32)
    return summed


def finish_kernel(
    merged_hbm, cot_hbm, p0, p1, p2, p3, coarse_out, grad_merged, merged, cot, parts, first, second, done
):
    copies = started(
        [(merged_hbm, merged, done.at[0]), (cot_hbm.at[0], cot, done.at[1])]
        + [(p, parts.at[j], done.at[2 + j]) for j, p in enumerate((p0, p1, p2, p3))]
    )
    for copy in copies:
        copy.wait()
    merged_f = merged[...].astype(F32)
    value, grad_normed = merged_f, 0.0
    for j in range(4):
        value = value + parts[j, 0].astype(F32)
        grad_normed = grad_normed + parts[j, 1].astype(F32)
    value = value.astype(BF16)
    centred = merged_f - jnp.mean(merged_f, axis=-1, keepdims=True)
    scale_inv = lax.rsqrt(jnp.mean(centred * centred, axis=-1, keepdims=True) + EPS)
    nhat = centred * scale_inv
    grad = cot[...].astype(F32) + scale_inv * (
        grad_normed
        - jnp.mean(grad_normed, axis=-1, keepdims=True)
        - nhat * jnp.mean(grad_normed * nhat, axis=-1, keepdims=True)
    )
    grad = grad.astype(BF16)
    for lat in range(6):
        for lon in range(3):
            rows = slice(6 * lat + 2 * lon, 6 * lat + 2 * lon + 2)
            first[lat, lon] = value[rows]
            second[lat, lon] = grad[rows]
    copies = started([(first, coarse_out, done.at[0]), (second, grad_merged, done.at[1])])
    for copy in copies:
        copy.wait()


def finish(*args):
    tokens = shaped((6, 3, 2, 1024))
    return call(
        finish_kernel, (tokens, tokens), *args, hbm=range(6), hbm_out=2, flops=10**11,
        scratch_shapes=[
            pltpu.VMEM((ROWS, 1024), BF16),
            pltpu.VMEM((ROWS, 1024), BF16),
            pltpu.VMEM((4, 2, ROWS, 1024), BF16),
            pltpu.VMEM(tokens.shape, BF16),
            pltpu.VMEM(tokens.shape, BF16),
            pltpu.SemaphoreType.DMA((6,)),
        ],
    )


def weight_kernel(place, cots, bundle, other, slope, result, slope_hbm, held, done):
    copies = started([(slope, slope_hbm, done.at[2])])
    at = pl.ds(pl.multiple_of(place[0] * 512, 512), 512)
    rows = jnp.concatenate([stacked_rows(cots, at), other[:, 1024:1536]], axis=0)
    hidden = jnp.concatenate([bundle[:, 0:1024], other[:, 0:1024]], axis=0)
    for z_hi in range(2):
        total = dot_tn(rows[:, 256 * z_hi : 256 * z_hi + 256], hidden).astype(BF16)
        held[z_hi] = total.reshape(16, 16, 1024)
        copies += started([(held.at[z_hi], result.at[:, 16 * z_hi : 16 * z_hi + 16, :], done.at[z_hi])])
    for copy in copies:
        copy.wait()


def plane_sum_kernel(place, parts, result, total):
    total[...] = sum_of(parts)
    for z_hi in range(2):
        for half in range(2):
            at = pl.ds(pl.multiple_of((place[3] ^ half) * 512, 512), 512)
            result[2 * z_hi + half] = total[16 * z_hi : 16 * z_hi + 16, at].astype(BF16)


def line_sum_kernel(parts, result):
    result[...] = sum_of(parts)


def on_device(fine_tokens, fine_qkv, fine_out, merge_weight, up_weight, down_weight, cotangent):
    place = jnp.stack([lax.axis_index(a) for a in ("lat", "y", "x", "z_half", "z_near")]).astype(jnp.int32)
    side0, side1, piece, cot = prepare(fine_tokens, cotangent, merge_weight, up_weight, down_weight)

    got0 = swapped(side0, 1)
    got1 = moved(side1, lambda s: (s + 1 if s % 2 else s - 1) % COUNT)
    piece = along_z(piece)

    cots = exchanged(cot, "z_near")
    tokens, own = call(
        project_kernel, (shaped((144, 512)), shaped((144, 1536))), side0, side1, fine_qkv, hbm=range(2),
        flops=2 * 10**8, after=(cots,),
        scratch_shapes=[
            pltpu.VMEM((72, 512), BF16),
            pltpu.VMEM((96, 512), BF16),
            pltpu.SemaphoreType.DMA((2,)),
        ],
    )
    merged_in = call(
        attend_kernel, shaped((ROWS, 2048)), place, tokens, own, got0, got1, fine_qkv, fine_out,
        jnp.asarray(merge_order()), scalars=1, hbm_out=1, flops=10**9,
        scratch_shapes=[pltpu.VMEM((ROWS, 2048), BF16), pltpu.SemaphoreType.DMA],
    )
    pieces = call(
        spread_kernel, shaped((16, 80, 512)), piece, hbm_out=1, after=(merged_in,),
        scratch_shapes=[pltpu.SemaphoreType.DMA((16,))],
    )
    near = exchanged(pieces, ("y", "x"))
    ins = [merged_in] + [swapped(merged_in, j) for j in (3, 2, 1)][::-1]
    near = call(copy_kernel, shaped((16, 80, 512)), near, after=(merged_in,))
    far = across(near)
    narrow = shaped((4 * ROWS, 128), F32)
    rows, own, part = call(
        merge_near_kernel, (shaped((4 * ROWS, 2048)), narrow, narrow),
        place, *ins, merge_weight, near, scalars=1, hbm=(1,), flops=10**11,
        scratch_shapes=[
            pltpu.VMEM((ROWS, 2048), BF16),
            pltpu.VMEM((1024, 128), BF16),
            pltpu.SemaphoreType.DMA,
        ],
    )
    columns = call(
        merge_kernel, shaped((4, 4, ROWS, 256)), place, rows, own, part, far, scalars=1, flops=10**8,
        scratch_shapes=[pltpu.VMEM((1024, 128), BF16)],
    )
    columns = exchanged(columns, "z_near")
    own_merged, slope, bundle = call(
        hidden_kernel,
        (shaped((ROWS, 1024)), shaped((4 * ROWS, 1024), F32), shaped((4 * ROWS, 1536))),
        place, up_weight, columns, cots, near, far, scalars=1, hbm=(1,), hbm_out=1, flops=10**9,
        scratch_shapes=[
            pltpu.VMEM((4 * ROWS, 1024), F32),
            pltpu.VMEM((ROWS, 1024), BF16),
            pltpu.VMEM((4 * ROWS, 1024), BF16),
            pltpu.VMEM((1024, 512), BF16),
            pltpu.SemaphoreType.DMA((2,)),
        ],
    )
    other = across(bundle)
    parts, slope = call(
        weight_kernel, (shaped((16, 32, 1024)), shaped((4 * ROWS, 1024), F32)), place, cots, bundle, other, slope,
        scalars=1, hbm_out=2, flops=3 * 10**8,
        scratch_shapes=[pltpu.VMEM((2, 16, 16, 1024), BF16), pltpu.SemaphoreType.DMA((3,))],
    )
    parts = exchanged(parts, ("y", "x"))
    partial = shaped((2, ROWS, 1024))
    partials = call(
        feed_kernel, (partial,) * 4, place, up_weight, down_weight, slope, bundle, cots, near, far, scalars=1,
        hbm=range(1, 4), hbm_out=4, flops=2 * 10**9,
        scratch_shapes=[
            pltpu.VMEM((4 * ROWS, 1024), F32),
            pltpu.VMEM((4 * ROWS, 1024), F32),
            pltpu.VMEM((4, 2, ROWS, 1024), BF16),
            pltpu.VMEM((1024, 512), BF16),
            pltpu.VMEM((512, 1024), BF16),
            pltpu.VMEM((4 * ROWS, 1024), F32),
            pltpu.SemaphoreType.DMA((7,)),
        ],
    )
    partials = [partials[0]] + [swapped(partials[j], j) for j in (3, 2, 1)][::-1]
    parts = call(
        plane_sum_kernel, shaped((4, 16, 512)), place, parts, scalars=1,
        scratch_shapes=[pltpu.VMEM((32, 1024), F32)],
    )
    parts = exchanged(parts, ("z_hi", "z_half"))
    coarse_out, grad_merged = finish(own_merged, cot, *partials)
    grad_down, coarse_out, grad_merged = call(
        line_sum_kernel, shaped((16, 512), F32), parts, through=(coarse_out, grad_merged)
    )
    grad_down = grad_down.T
    return coarse_out.transpose(2, 0, 1, 3), grad_merged.transpose(2, 0, 1, 3), grad_down


def solution(mesh):
    lon, tp = ("z_hi", "y", "x"), ("z_half", "z_near")
    parts = Mesh(mesh.devices.reshape(2, 2, 4, 4, 2, 4), AXES)
    tokens = P(None, "lat", lon + tp, None)
    return jax.shard_map(
        on_device,
        mesh=parts,
        in_specs=(tokens, P(), P(), P(None, tp), P(None, tp), P(tp, None), tokens),
        out_specs=(tokens, tokens, P(tp, ("lat",) + lon)),
        check_vma=False,
    )
```

```python
import jax
import jax.numpy as jnp
import numpy as np
from jax import lax
from jax.experimental import pallas as pl
from jax.experimental.pallas import tpu as pltpu
from jax.sharding import Mesh, PartitionSpec as P

EPS = 1e-05
F32 = jnp.float32
BF16 = jnp.bfloat16
AXES = ("lat", "z_hi", "y", "x", "z_half", "z_near")
LINE = AXES[1:]
COUNT = 256
ROWS = 40


def dot(a, b):
    return lax.dot_general(a, b, (((1,), (0,)), ((), ())), preferred_element_type=F32)


def dot_nt(a, b):
    return lax.dot_general(a, b, (((1,), (1,)), ((), ())), preferred_element_type=F32)


def dot_tn(a, b):
    return lax.dot_general(a, b, (((0,), (0,)), ((), ())), preferred_element_type=F32)


def moved(value, target):
    return lax.ppermute(value, LINE, [(s, target(s)) for s in range(COUNT)])


def swapped(value, bits):
    return moved(value, lambda s: s ^ bits)


def across(value):
    return lax.ppermute(value, "lat", [(0, 1), (1, 0)])


def along_z(value):
    pairs = []
    for lat, steps in ((0, 4), (1, -4)):
        for lon in range(32):
            for tp in range(8):
                z = ((lon >> 4) * 8 + tp + steps) % 16
                target = (z >> 3) * 128 + (lon & 15) * 8 + (z & 7)
                pairs.append((lat * COUNT + lon * 8 + tp, lat * COUNT + target))
    return lax.ppermute(value, AXES, pairs)


def exchanged(value, axes):
    return lax.all_to_all(value, axes, 0, 0)


def norm_rows(values):
    centred = values - jnp.mean(values, axis=-1, keepdims=True)
    variance = jnp.mean(centred * centred, axis=-1, keepdims=True)
    return centred * lax.rsqrt(variance + EPS)


def in_hbm(value):
    return pltpu.with_memory_space_constraint(value, pltpu.HBM)


def call(kernel, out_shape, *args, flops=0, scalars=0, hbm=(), hbm_out=0, after=(), through=(), limit=16, **kw):
    outs = out_shape if isinstance(out_shape, tuple) else (out_shape,)
    here, far = pl.BlockSpec(memory_space=pltpu.VMEM), pl.BlockSpec(memory_space=pltpu.HBM)
    scalar = pl.BlockSpec(memory_space=pltpu.SMEM)
    specs = [scalar if i < scalars else far if i in hbm else here for i in range(len(args))]
    first, last = len(args) + len(after), len(args) + len(after) + len(through)

    def body(*refs):
        kernel(*refs[: len(args)], *refs[last : last + len(outs)], *refs[last + len(outs) + len(through) :])

    size = sum(a.size * a.dtype.itemsize for a in args)
    result = pl.pallas_call(
        body,
        out_shape=tuple(pltpu.HBM(o.shape, o.dtype) if i < hbm_out else o for i, o in enumerate(outs))
        + tuple(pltpu.HBM(t.shape, t.dtype) for t in through),
        in_specs=specs + [far] * (len(after) + len(through)),
        out_specs=(far,) * hbm_out + (here,) * (len(outs) - hbm_out) + (far,) * len(through),
        input_output_aliases={first + i: len(outs) + i for i in range(len(through))},
        compiler_params=pltpu.CompilerParams(vmem_limit_bytes=limit * 1024 * 1024) if limit else None,
        cost_estimate=pl.CostEstimate(flops=flops, bytes_accessed=size, transcendentals=0),
        name=kernel.__name__,
        **kw,
    )(*(in_hbm(a) if i in hbm else a for i, a in enumerate(args)), *(in_hbm(a) for a in (*after, *through)))
    return result if len(result) > 1 else result[0]


def shaped(shape, dtype=BF16):
    return jax.ShapeDtypeStruct(shape, dtype)


def merge_order():
    order = np.zeros((2, 4 * ROWS, 144), np.float32)
    for odd in range(2):
        for quarter in range(4):
            d_lat, d_lon = quarter // 2, quarter % 2
            for token in range(36):
                lat, lon, lev = token // 6, token % 6 // 2, token % 2
                row, column = 2 * lat + d_lat, 2 * lon + d_lon
                side = column // 3 if odd else 1 - column // 3
                order[odd, ROWS * quarter + token, 72 * side + 6 * row + 2 * (column % 3) + lev] = 1.0
    return order.astype(jnp.bfloat16)


def started(copies):
    copies = [pltpu.make_async_copy(*c) for c in copies]
    for copy in copies:
        copy.start()
    return copies


def project_kernel(side0, side1, qkv, tokens, packed, held0, held1, done):
    for copy in started([(side0, held0, done.at[0]), (side1, held1, done.at[1])]):
        copy.wait()
    rows = jnp.concatenate([held0[...].astype(F32), held1[0:72].astype(F32)], axis=0)
    tokens[...] = rows.astype(BF16)
    packed[...] = dot(norm_rows(rows).astype(BF16), qkv[...]).astype(BF16)


def attend_kernel(place, own_tokens, own, got0, got1, qkv, out_w, order, result, merged_in, done):
    tokens = own_tokens[...].astype(F32)
    others = jnp.concatenate([got0[...].astype(F32), got1[0:72].astype(F32)], axis=0)
    other_packed = dot(norm_rows(others).astype(BF16), qkv[:, 512:1536]).astype(BF16).astype(F32)
    packed = own[...].astype(F32)
    lane = lax.broadcasted_iota(jnp.int32, (1, 128), 1) // 32
    masks = [(lane == h).astype(F32) for h in range(4)]
    scale = 32 ** -0.5
    halves = []
    for window in range(2):
        rows = slice(72 * window, 72 * window + 72)
        parts = []
        for group in range(4):
            low = 128 * group
            queries = packed[rows, low : low + 128]
            keys = jnp.concatenate(
                [packed[rows, 512 + low : 640 + low], other_packed[rows, low : low + 128]], axis=0
            ).astype(BF16)
            values = jnp.concatenate(
                [packed[rows, 1024 + low : 1152 + low], other_packed[rows, 512 + low : 640 + low]], axis=0
            ).astype(BF16)
            stacked = jnp.concatenate([queries * m for m in masks], axis=0).astype(BF16)
            scores = dot_nt(stacked, keys) * scale
            scores = scores - jnp.max(scores, axis=-1, keepdims=True)
            scores = jnp.exp(scores)
            probs = (scores / jnp.sum(scores, axis=-1, keepdims=True)).astype(BF16)
            mixed = dot(probs, values)
            total = mixed[0:72] * masks[0]
            for h in range(1, 4):
                total = total + mixed[72 * h : 72 * h + 72] * masks[h]
            parts.append(total)
        halves.append(jnp.concatenate(parts, axis=1))
    mixed = jnp.concatenate(halves, axis=0).astype(BF16)
    section = (tokens + dot(mixed, out_w[...])).astype(BF16)
    spread = dot(order[place[4] & 1], section)
    wide = jnp.concatenate([spread[ROWS * q : ROWS * q + ROWS] for q in range(4)], axis=1)
    merged_in[...] = norm_rows(wide).astype(BF16)
    for copy in started([(merged_in, result, done)]):
        copy.wait()


def stacked_rows(blocks, columns):
    return jnp.concatenate([blocks[j, :, columns].astype(F32) for j in range(4)], axis=0).astype(BF16)


def merge_half(place, source, side, weight):
    for index in range(16):
        for q in range(4):
            weight[64 * index + 16 * q : 64 * index + 16 * q + 16, :] = source[index, 64:80, 128 * q : 128 * q + 128]
    return pl.ds(pl.multiple_of((place[0] ^ side) * 1024, 1024), 1024)


def merge_near_kernel(place, own_in, b1, b2, b3, own_w, near, rows, own, part, held, weight, done):
    (copy,) = started([(own_in, held, done)])
    at = merge_half(place, near, 0, weight)
    copy.wait()
    rows[...] = jnp.concatenate([b[...].astype(F32) for b in (held, b1, b2, b3)], axis=0).astype(BF16)
    own[...] = dot(rows[...], own_w[...])
    part[...] = dot(rows[:, at], weight[...])


def merge_kernel(place, rows, own, part, far, result, weight):
    at = merge_half(place, far, 1, weight)
    for half, part in enumerate((own[...], part[...] + dot(rows[:, at], weight[...]))):
        for j in range(4):
            result[place[4] ^ j, :, 128 * half : 128 * half + 128] = part[ROWS * j : ROWS * j + ROWS].astype(BF16)


def prepare_kernel(
    tokens, cotangent, merge, up, down, side0, side1, packed, cot, tokens_in, cot_in, done
):
    r = lax.axis_index("lat") * 16 + lax.axis_index("y") * 4 + lax.axis_index("x")
    east = 1 - (lax.axis_index("z_near") & 1)
    pairs = [
        (tokens, tokens_in),
        (cotangent, cot_in),
        (up.at[pl.ds(pl.multiple_of(r * 32, 32), 32), :], packed.at[0:32, :]),
    ]
    row = pl.ds(pl.multiple_of(r * 16, 16), 16)
    for half in range(2):
        pairs.append((down.at[row, 512 * half : 512 * half + 512], packed.at[32 + 16 * half : 48 + 16 * half, :]))
    for q in range(4):
        at = pl.ds(pl.multiple_of(r * 64 + 16 * q, 16), 16)
        pairs.append((merge.at[at, :], packed.at[64:80, 128 * q : 128 * q + 128]))
    copies = started([(a, b, done.at[i]) for i, (a, b) in enumerate(pairs)])
    copies[0].wait()
    for lat in range(12):
        for lon in range(3):
            rows = slice(6 * lat + 2 * lon, 6 * lat + 2 * lon + 2)
            side0[rows, :] = tokens_in[lat, 3 * east + lon]
            side1[rows, :] = tokens_in[lat, 3 * (1 - east) + lon]
    side1[72:96, :] = jnp.zeros((24, 512), BF16)
    copies[1].wait()
    for copy in range(4):
        for lat in range(6):
            for lon in range(3):
                cot[copy, 6 * lat + 2 * lon : 6 * lat + 2 * lon + 2, :] = cot_in[lat, lon]
        cot[copy, 36:40, :] = jnp.zeros((4, 1024), BF16)
    for copy in copies[2:]:
        copy.wait()


def prepare(tokens, cotangent, merge, up, down):
    hbm = pl.BlockSpec(memory_space=pltpu.HBM)
    vmem = pl.BlockSpec(memory_space=pltpu.VMEM)
    return pl.pallas_call(
        prepare_kernel,
        out_shape=(shaped((72, 512)), shaped((96, 512)), shaped((80, 512)), shaped((4, ROWS, 1024))),
        in_specs=[hbm] * 5,
        out_specs=(vmem,) * 4,
        scratch_shapes=[
            pltpu.VMEM((12, 6, 2, 512), BF16),
            pltpu.VMEM((6, 3, 2, 1024), BF16),
            pltpu.SemaphoreType.DMA((9,)),
        ],
        name="prepare_kernel",
    )(tokens.transpose(1, 2, 0, 3), cotangent.transpose(1, 2, 0, 3), merge, up, down)


def spread_kernel(piece, result, done):
    for copy in started([(piece, result.at[i], done.at[i]) for i in range(16)]):
        copy.wait()


def after_kernel(result):
    result[...] = jnp.zeros(result.shape, F32)


def copy_kernel(source, result):
    result[...] = source[...]


def up_half(source):
    return source[:, 0:32, :].reshape(512, 512)


def down_half(source, columns):
    return source[:, 32 + 16 * columns : 48 + 16 * columns, :].reshape(256, 512)


def gelu_parts(values):
    cdf = 0.5 * (1.0 + lax.erf(values * np.float32(np.sqrt(0.5))))
    density = jnp.exp(-0.5 * values * values) * np.float32(1.0 / np.sqrt(2.0 * np.pi))
    return values * cdf, cdf + values * density


def hidden_kernel(
    place, up_hbm, m0, m1, m2, m3, cots, near, far, own_merged, slope, bundle, merged, own, normed, up, done
):
    (fetch,) = started([(up_hbm, up, done.at[1])])
    lat, half_index, near_index = place[0], place[3], place[4]
    for j, columns in enumerate((m0, m1, m2, m3)):
        for half in range(2):
            column = pl.multiple_of(((half_index ^ half) * 4 + (near_index ^ j)) * 128, 128)
            for block in range(4):
                merged[ROWS * block : ROWS * block + ROWS, pl.ds(column, 128)] = columns[
                    block, :, 128 * half : 128 * half + 128
                ].astype(F32)
    own[...] = merged[pl.ds(pl.multiple_of(near_index * ROWS, 8), ROWS), :].astype(BF16)
    (copy,) = started([(own, own_merged, done.at[0])])
    normed[...] = norm_rows(merged[...]).astype(BF16)
    fetch.wait()
    value, slope[:, 0:512] = gelu_parts(dot(normed[...], up[...]))
    bundle[:, 0:512] = value.astype(BF16)
    preact = 0.0
    for side, source in enumerate((near, far)):
        at = pl.ds(pl.multiple_of((lat ^ side) * 512, 512), 512)
        preact = preact + dot(normed[:, at], up_half(source))
    value, slope[:, 512:1024] = gelu_parts(preact)
    bundle[:, 512:1024] = value.astype(BF16)
    bundle[:, 1024:1536] = stacked_rows(cots, pl.ds(pl.multiple_of((1 - lat) * 512, 512), 512))
    copy.wait()


def feed_kernel(
    place, up_hbm, down_hbm, slope_hbm, bundle, cots, near, far, s0, s1, s2, s3,
    values, grads, parts, up, down, slope, done,
):
    copies = started([(slope_hbm, slope, done.at[0]), (down_hbm, down, done.at[1]), (up_hbm, up, done.at[2])])
    cots = stacked_rows(cots, slice(0, 1024))
    far_values, far_hidden, far_grads = [0.0, 0.0], [], []
    for side, source in enumerate((near, far)):
        at = pl.ds(pl.multiple_of(512 + (place[0] ^ side) * 256, 256), 256)
        units = bundle[:, at]
        grad = 0.0
        for half in range(2):
            part = down_half(source, half)
            far_values[half] = far_values[half] + dot(units, part)
            grad = grad + dot_nt(cots[:, 512 * half : 512 * half + 512], part)
        far_hidden.append(grad)
    copies[0].wait()
    for side, grad in enumerate(far_hidden):
        at = pl.ds(pl.multiple_of(512 + (place[0] ^ side) * 256, 256), 256)
        far_grads.append((grad * slope[:, at]).astype(BF16))
    copies[1].wait()
    own_grad = (dot_nt(cots, down[...]) * slope[:, 0:512]).astype(BF16)
    values[...] = dot(bundle[:, 0:512], down[...]) + jnp.concatenate(far_values, axis=1)
    copies[2].wait()
    grads[...] = dot_nt(own_grad, up[...])
    first = jnp.where(place[0] == 0, far_grads[0].astype(F32), far_grads[1].astype(F32)).astype(BF16)
    second = jnp.where(place[0] == 0, far_grads[1].astype(F32), far_grads[0].astype(F32)).astype(BF16)
    grad = jnp.concatenate([first, second], axis=1)
    for side, source in enumerate((near, far)):
        at = pl.ds(pl.multiple_of((place[0] ^ side) * 512, 512), 512)
        grads[:, at] = grads[:, at] + dot_nt(grad, up_half(source))
    copies = []
    for j, sent in reversed(list(enumerate((s0, s1, s2, s3)))):
        at = pl.ds(pl.multiple_of((place[4] ^ j) * ROWS, 8), ROWS)
        parts[j, 0] = values[at, :].astype(BF16)
        parts[j, 1] = grads[at, :].astype(BF16)
        copies += started([(parts.at[j], sent, done.at[3 + j])])
    for copy in copies:
        copy.wait()


def sum_of(parts):
    summed = parts[0].astype(F32)
    for index in range(1, parts.shape[0]):
        summed = summed + parts[index].astype(F32)
    return summed


def finish_kernel(
    merged_hbm, cot_hbm, p0, p1, p2, p3, coarse_out, grad_merged, merged, cot, parts, first, second, done
):
    copies = started(
        [(merged_hbm, merged, done.at[0]), (cot_hbm.at[0], cot, done.at[1])]
        + [(p, parts.at[j], done.at[2 + j]) for j, p in enumerate((p0, p1, p2, p3))]
    )
    for copy in copies:
        copy.wait()
    merged_f = merged[...].astype(F32)
    value, grad_normed = merged_f, 0.0
    for j in range(4):
        value = value + parts[j, 0].astype(F32)
        grad_normed = grad_normed + parts[j, 1].astype(F32)
    value = value.astype(BF16)
    centred = merged_f - jnp.mean(merged_f, axis=-1, keepdims=True)
    scale_inv = lax.rsqrt(jnp.mean(centred * centred, axis=-1, keepdims=True) + EPS)
    nhat = centred * scale_inv
    grad = cot[...].astype(F32) + scale_inv * (
        grad_normed
        - jnp.mean(grad_normed, axis=-1, keepdims=True)
        - nhat * jnp.mean(grad_normed * nhat, axis=-1, keepdims=True)
    )
    grad = grad.astype(BF16)
    for lat in range(6):
        for lon in range(3):
            rows = slice(6 * lat + 2 * lon, 6 * lat + 2 * lon + 2)
            first[lat, lon] = value[rows]
            second[lat, lon] = grad[rows]
    copies = started([(first, coarse_out, done.at[0]), (second, grad_merged, done.at[1])])
    for copy in copies:
        copy.wait()


def finish(*args):
    tokens = shaped((6, 3, 2, 1024))
    return call(
        finish_kernel, (tokens, tokens), *args, hbm=range(6), hbm_out=2, flops=10**11,
        scratch_shapes=[
            pltpu.VMEM((ROWS, 1024), BF16),
            pltpu.VMEM((ROWS, 1024), BF16),
            pltpu.VMEM((4, 2, ROWS, 1024), BF16),
            pltpu.VMEM(tokens.shape, BF16),
            pltpu.VMEM(tokens.shape, BF16),
            pltpu.SemaphoreType.DMA((6,)),
        ],
    )


def weight_kernel(place, cots, bundle, other, slope, result, slope_hbm, held, done):
    copies = started([(slope, slope_hbm, done.at[2])])
    at = pl.ds(pl.multiple_of(place[0] * 512, 512), 512)
    rows = jnp.concatenate([stacked_rows(cots, at), other[:, 1024:1536]], axis=0)
    hidden = jnp.concatenate([bundle[:, 0:1024], other[:, 0:1024]], axis=0)
    for z_hi in range(2):
        total = dot_tn(rows[:, 256 * z_hi : 256 * z_hi + 256], hidden).astype(BF16)
        held[z_hi] = total.reshape(16, 16, 1024)
        copies += started([(held.at[z_hi], result.at[:, 16 * z_hi : 16 * z_hi + 16, :], done.at[z_hi])])
    for copy in copies:
        copy.wait()


def plane_sum_kernel(place, parts, result, total):
    total[...] = sum_of(parts)
    for z_hi in range(2):
        for half in range(2):
            at = pl.ds(pl.multiple_of((place[3] ^ half) * 512, 512), 512)
            result[2 * z_hi + half] = total[16 * z_hi : 16 * z_hi + 16, at].astype(BF16)


def line_sum_kernel(parts, result):
    result[...] = sum_of(parts)


def on_device(fine_tokens, fine_qkv, fine_out, merge_weight, up_weight, down_weight, cotangent):
    place = jnp.stack([lax.axis_index(a) for a in ("lat", "y", "x", "z_half", "z_near")]).astype(jnp.int32)
    side0, side1, piece, cot = prepare(fine_tokens, cotangent, merge_weight, up_weight, down_weight)

    got0 = swapped(side0, 1)
    got1 = moved(side1, lambda s: (s + 1 if s % 2 else s - 1) % COUNT)
    piece = along_z(piece)

    cots = exchanged(cot, "z_near")
    tokens, own = call(
        project_kernel, (shaped((144, 512)), shaped((144, 1536))), side0, side1, fine_qkv, hbm=range(2),
        flops=2 * 10**8, after=(cots,),
        scratch_shapes=[
            pltpu.VMEM((72, 512), BF16),
            pltpu.VMEM((96, 512), BF16),
            pltpu.SemaphoreType.DMA((2,)),
        ],
    )
    merged_in = call(
        attend_kernel, shaped((ROWS, 2048)), place, tokens, own, got0, got1, fine_qkv, fine_out,
        jnp.asarray(merge_order()), scalars=1, hbm_out=1, flops=10**9,
        scratch_shapes=[pltpu.VMEM((ROWS, 2048), BF16), pltpu.SemaphoreType.DMA],
    )
    pieces = call(
        spread_kernel, shaped((16, 80, 512)), piece, hbm_out=1, after=(merged_in,),
        scratch_shapes=[pltpu.SemaphoreType.DMA((16,))],
    )
    near = exchanged(pieces, ("y", "x"))
    ins = [merged_in] + [swapped(merged_in, j) for j in (3, 2, 1)][::-1]
    near = call(copy_kernel, shaped((16, 80, 512)), near, after=(merged_in,))
    far = across(near)
    narrow = shaped((4 * ROWS, 128), F32)
    rows, own, part = call(
        merge_near_kernel, (shaped((4 * ROWS, 2048)), narrow, narrow),
        place, *ins, merge_weight, near, scalars=1, hbm=(1,), flops=10**11,
        scratch_shapes=[
            pltpu.VMEM((ROWS, 2048), BF16),
            pltpu.VMEM((1024, 128), BF16),
            pltpu.SemaphoreType.DMA,
        ],
    )
    columns = call(
        merge_kernel, shaped((4, ROWS, 256)), place, rows, own, part, far, scalars=1, flops=10**8,
        scratch_shapes=[pltpu.VMEM((1024, 128), BF16)],
    )
    columns = [columns] + [swapped(columns, j) for j in (3, 2, 1)][::-1]
    own_merged, slope, bundle = call(
        hidden_kernel,
        (shaped((ROWS, 1024)), shaped((4 * ROWS, 1024), F32), shaped((4 * ROWS, 1536))),
        place, up_weight, *columns, cots, near, far, scalars=1, hbm=(1,), hbm_out=1, flops=10**9,
        scratch_shapes=[
            pltpu.VMEM((4 * ROWS, 1024), F32),
            pltpu.VMEM((ROWS, 1024), BF16),
            pltpu.VMEM((4 * ROWS, 1024), BF16),
            pltpu.VMEM((1024, 512), BF16),
            pltpu.SemaphoreType.DMA((2,)),
        ],
    )
    other = across(bundle)
    parts, slope = call(
        weight_kernel, (shaped((16, 32, 1024)), shaped((4 * ROWS, 1024), F32)), place, cots, bundle, other, slope,
        scalars=1, hbm_out=2, flops=3 * 10**8,
        scratch_shapes=[pltpu.VMEM((2, 16, 16, 1024), BF16), pltpu.SemaphoreType.DMA((3,))],
    )
    parts = exchanged(parts, ("y", "x"))
    partial = shaped((2, ROWS, 1024))
    partials = call(
        feed_kernel, (partial,) * 4, place, up_weight, down_weight, slope, bundle, cots, near, far, scalars=1,
        hbm=range(1, 4), hbm_out=4, flops=2 * 10**9,
        scratch_shapes=[
            pltpu.VMEM((4 * ROWS, 1024), F32),
            pltpu.VMEM((4 * ROWS, 1024), F32),
            pltpu.VMEM((4, 2, ROWS, 1024), BF16),
            pltpu.VMEM((1024, 512), BF16),
            pltpu.VMEM((512, 1024), BF16),
            pltpu.VMEM((4 * ROWS, 1024), F32),
            pltpu.SemaphoreType.DMA((7,)),
        ],
    )
    partials = [partials[0]] + [swapped(partials[j], j) for j in (3, 2, 1)][::-1]
    parts = call(
        plane_sum_kernel, shaped((4, 16, 512)), place, parts, scalars=1,
        scratch_shapes=[pltpu.VMEM((32, 1024), F32)],
    )
    parts = exchanged(parts, ("z_hi", "z_half"))
    coarse_out, grad_merged = finish(own_merged, cot, *partials)
    grad_down, coarse_out, grad_merged = call(
        line_sum_kernel, shaped((16, 512), F32), parts, through=(coarse_out, grad_merged)
    )
    grad_down = grad_down.T
    return coarse_out.transpose(2, 0, 1, 3), grad_merged.transpose(2, 0, 1, 3), grad_down


def solution(mesh):
    lon, tp = ("z_hi", "y", "x"), ("z_half", "z_near")
    parts = Mesh(mesh.devices.reshape(2, 2, 4, 4, 2, 4), AXES)
    tokens = P(None, "lat", lon + tp, None)
    return jax.shard_map(
        on_device,
        mesh=parts,
        in_specs=(tokens, P(), P(), P(None, tp), P(None, tp), P(tp, None), tokens),
        out_specs=(tokens, tokens, P(tp, ("lat",) + lon)),
        check_vma=False,
    )
```

```python
import jax
import jax.numpy as jnp
import numpy as np
from jax import lax
from jax.experimental import pallas as pl
from jax.experimental.pallas import tpu as pltpu
from jax.sharding import Mesh, PartitionSpec as P

EPS = 1e-05
F32 = jnp.float32
BF16 = jnp.bfloat16
AXES = ("lat", "z_hi", "y", "x", "z_half", "z_near")
LINE = AXES[1:]
COUNT = 256
ROWS = 40


def dot(a, b):
    return lax.dot_general(a, b, (((1,), (0,)), ((), ())), preferred_element_type=F32)


def dot_nt(a, b):
    return lax.dot_general(a, b, (((1,), (1,)), ((), ())), preferred_element_type=F32)


def dot_tn(a, b):
    return lax.dot_general(a, b, (((0,), (0,)), ((), ())), preferred_element_type=F32)


def moved(value, target):
    return lax.ppermute(value, LINE, [(s, target(s)) for s in range(COUNT)])


def swapped(value, bits):
    return moved(value, lambda s: s ^ bits)


def across(value):
    return lax.ppermute(value, "lat", [(0, 1), (1, 0)])


def along_z(value):
    pairs = []
    for lat, steps in ((0, 4), (1, -4)):
        for lon in range(32):
            for tp in range(8):
                z = ((lon >> 4) * 8 + tp + steps) % 16
                target = (z >> 3) * 128 + (lon & 15) * 8 + (z & 7)
                pairs.append((lat * COUNT + lon * 8 + tp, lat * COUNT + target))
    return lax.ppermute(value, AXES, pairs)


def exchanged(value, axes):
    return lax.all_to_all(value, axes, 0, 0)


def norm_rows(values):
    centred = values - jnp.mean(values, axis=-1, keepdims=True)
    variance = jnp.mean(centred * centred, axis=-1, keepdims=True)
    return centred * lax.rsqrt(variance + EPS)


def in_hbm(value):
    return pltpu.with_memory_space_constraint(value, pltpu.HBM)


def call(kernel, out_shape, *args, flops=0, scalars=0, hbm=(), hbm_out=0, after=(), through=(), limit=16, **kw):
    outs = out_shape if isinstance(out_shape, tuple) else (out_shape,)
    here, far = pl.BlockSpec(memory_space=pltpu.VMEM), pl.BlockSpec(memory_space=pltpu.HBM)
    scalar = pl.BlockSpec(memory_space=pltpu.SMEM)
    specs = [scalar if i < scalars else far if i in hbm else here for i in range(len(args))]
    first, last = len(args) + len(after), len(args) + len(after) + len(through)

    def body(*refs):
        kernel(*refs[: len(args)], *refs[last : last + len(outs)], *refs[last + len(outs) + len(through) :])

    size = sum(a.size * a.dtype.itemsize for a in args)
    result = pl.pallas_call(
        body,
        out_shape=tuple(pltpu.HBM(o.shape, o.dtype) if i < hbm_out else o for i, o in enumerate(outs))
        + tuple(pltpu.HBM(t.shape, t.dtype) for t in through),
        in_specs=specs + [far] * (len(after) + len(through)),
        out_specs=(far,) * hbm_out + (here,) * (len(outs) - hbm_out) + (far,) * len(through),
        input_output_aliases={first + i: len(outs) + i for i in range(len(through))},
        compiler_params=pltpu.CompilerParams(vmem_limit_bytes=limit * 1024 * 1024) if limit else None,
        cost_estimate=pl.CostEstimate(flops=flops, bytes_accessed=size, transcendentals=0),
        name=kernel.__name__,
        **kw,
    )(*(in_hbm(a) if i in hbm else a for i, a in enumerate(args)), *(in_hbm(a) for a in (*after, *through)))
    return result if len(result) > 1 else result[0]


def shaped(shape, dtype=BF16):
    return jax.ShapeDtypeStruct(shape, dtype)


def merge_order():
    order = np.zeros((2, 4 * ROWS, 144), np.float32)
    for odd in range(2):
        for quarter in range(4):
            d_lat, d_lon = quarter // 2, quarter % 2
            for token in range(36):
                lat, lon, lev = token // 6, token % 6 // 2, token % 2
                row, column = 2 * lat + d_lat, 2 * lon + d_lon
                side = column // 3 if odd else 1 - column // 3
                order[odd, ROWS * quarter + token, 72 * side + 6 * row + 2 * (column % 3) + lev] = 1.0
    return order.astype(jnp.bfloat16)


def started(copies):
    copies = [pltpu.make_async_copy(*c) for c in copies]
    for copy in copies:
        copy.start()
    return copies


def project_kernel(side0, side1, qkv, tokens, packed, held0, held1, done):
    for copy in started([(side0, held0, done.at[0]), (side1, held1, done.at[1])]):
        copy.wait()
    rows = jnp.concatenate([held0[...].astype(F32), held1[0:72].astype(F32)], axis=0)
    tokens[...] = rows.astype(BF16)
    packed[...] = dot(norm_rows(rows).astype(BF16), qkv[...]).astype(BF16)


def attend_kernel(place, own_tokens, own, got0, got1, qkv, out_w, order, result, merged_in, done):
    tokens = own_tokens[...].astype(F32)
    others = jnp.concatenate([got0[...].astype(F32), got1[0:72].astype(F32)], axis=0)
    other_packed = dot(norm_rows(others).astype(BF16), qkv[:, 512:1536]).astype(BF16).astype(F32)
    packed = own[...].astype(F32)
    lane = lax.broadcasted_iota(jnp.int32, (1, 128), 1) // 32
    masks = [(lane == h).astype(F32) for h in range(4)]
    scale = 32 ** -0.5
    halves = []
    for window in range(2):
        rows = slice(72 * window, 72 * window + 72)
        parts = []
        for group in range(4):
            low = 128 * group
            queries = packed[rows, low : low + 128]
            keys = jnp.concatenate(
                [packed[rows, 512 + low : 640 + low], other_packed[rows, low : low + 128]], axis=0
            ).astype(BF16)
            values = jnp.concatenate(
                [packed[rows, 1024 + low : 1152 + low], other_packed[rows, 512 + low : 640 + low]], axis=0
            ).astype(BF16)
            stacked = jnp.concatenate([queries * m for m in masks], axis=0).astype(BF16)
            scores = dot_nt(stacked, keys) * scale
            scores = scores - jnp.max(scores, axis=-1, keepdims=True)
            scores = jnp.exp(scores)
            probs = (scores / jnp.sum(scores, axis=-1, keepdims=True)).astype(BF16)
            mixed = dot(probs, values)
            total = mixed[0:72] * masks[0]
            for h in range(1, 4):
                total = total + mixed[72 * h : 72 * h + 72] * masks[h]
            parts.append(total)
        halves.append(jnp.concatenate(parts, axis=1))
    mixed = jnp.concatenate(halves, axis=0).astype(BF16)
    section = (tokens + dot(mixed, out_w[...])).astype(BF16)
    spread = dot(order[place[4] & 1], section)
    wide = jnp.concatenate([spread[ROWS * q : ROWS * q + ROWS] for q in range(4)], axis=1)
    merged_in[...] = norm_rows(wide).astype(BF16)
    for copy in started([(merged_in, result, done)]):
        copy.wait()


def stacked_rows(blocks, columns):
    return jnp.concatenate([blocks[j, :, columns].astype(F32) for j in range(4)], axis=0).astype(BF16)


def merge_half(place, source, side, weight):
    for index in range(16):
        for q in range(4):
            weight[64 * index + 16 * q : 64 * index + 16 * q + 16, :] = source[index, 64:80, 128 * q : 128 * q + 128]
    return pl.ds(pl.multiple_of((place[0] ^ side) * 1024, 1024), 1024)


def merge_near_kernel(place, own_in, b1, b2, b3, own_w, near, rows, own, part, held, weight, done):
    (copy,) = started([(own_in, held, done)])
    at = merge_half(place, near, 0, weight)
    copy.wait()
    rows[...] = jnp.concatenate([b[...].astype(F32) for b in (held, b1, b2, b3)], axis=0).astype(BF16)
    own[...] = dot(rows[...], own_w[...])
    part[...] = dot(rows[:, at], weight[...])


def merge_kernel(place, rows, own, part, far, result, weight):
    at = merge_half(place, far, 1, weight)
    for half, part in enumerate((own[...], part[...] + dot(rows[:, at], weight[...]))):
        for j in range(4):
            piece = part[ROWS * j : ROWS * j + ROWS].astype(BF16)
            for copy in range(4):
                result[copy, place[4] ^ j, :, 128 * half : 128 * half + 128] = piece


def prepare_kernel(
    tokens, cotangent, merge, up, down, side0, side1, packed, cot, tokens_in, cot_in, done
):
    r = lax.axis_index("lat") * 16 + lax.axis_index("y") * 4 + lax.axis_index("x")
    east = 1 - (lax.axis_index("z_near") & 1)
    pairs = [
        (tokens, tokens_in),
        (cotangent, cot_in),
        (up.at[pl.ds(pl.multiple_of(r * 32, 32), 32), :], packed.at[0:32, :]),
    ]
    row = pl.ds(pl.multiple_of(r * 16, 16), 16)
    for half in range(2):
        pairs.append((down.at[row, 512 * half : 512 * half + 512], packed.at[32 + 16 * half : 48 + 16 * half, :]))
    for q in range(4):
        at = pl.ds(pl.multiple_of(r * 64 + 16 * q, 16), 16)
        pairs.append((merge.at[at, :], packed.at[64:80, 128 * q : 128 * q + 128]))
    copies = started([(a, b, done.at[i]) for i, (a, b) in enumerate(pairs)])
    copies[0].wait()
    for lat in range(12):
        for lon in range(3):
            rows = slice(6 * lat + 2 * lon, 6 * lat + 2 * lon + 2)
            side0[rows, :] = tokens_in[lat, 3 * east + lon]
            side1[rows, :] = tokens_in[lat, 3 * (1 - east) + lon]
    side1[72:96, :] = jnp.zeros((24, 512), BF16)
    copies[1].wait()
    for copy in range(4):
        for lat in range(6):
            for lon in range(3):
                cot[copy, 6 * lat + 2 * lon : 6 * lat + 2 * lon + 2, :] = cot_in[lat, lon]
        cot[copy, 36:40, :] = jnp.zeros((4, 1024), BF16)
    for copy in copies[2:]:
        copy.wait()


def prepare(tokens, cotangent, merge, up, down):
    hbm = pl.BlockSpec(memory_space=pltpu.HBM)
    vmem = pl.BlockSpec(memory_space=pltpu.VMEM)
    return pl.pallas_call(
        prepare_kernel,
        out_shape=(shaped((72, 512)), shaped((96, 512)), shaped((80, 512)), shaped((4, ROWS, 1024))),
        in_specs=[hbm] * 5,
        out_specs=(vmem,) * 4,
        scratch_shapes=[
            pltpu.VMEM((12, 6, 2, 512), BF16),
            pltpu.VMEM((6, 3, 2, 1024), BF16),
            pltpu.SemaphoreType.DMA((9,)),
        ],
        name="prepare_kernel",
    )(tokens.transpose(1, 2, 0, 3), cotangent.transpose(1, 2, 0, 3), merge, up, down)


def spread_kernel(piece, result, done):
    for copy in started([(piece, result.at[i], done.at[i]) for i in range(16)]):
        copy.wait()


def after_kernel(result):
    result[...] = jnp.zeros(result.shape, F32)


def copy_kernel(source, result):
    result[...] = source[...]


def up_half(source):
    return source[:, 0:32, :].reshape(512, 512)


def down_half(source, columns):
    return source[:, 32 + 16 * columns : 48 + 16 * columns, :].reshape(256, 512)


def gelu_parts(values):
    cdf = 0.5 * (1.0 + lax.erf(values * np.float32(np.sqrt(0.5))))
    density = jnp.exp(-0.5 * values * values) * np.float32(1.0 / np.sqrt(2.0 * np.pi))
    return values * cdf, cdf + values * density


def hidden_kernel(
    place, up_hbm, columns, cots, near, far, own_merged, slope, bundle, merged, own, normed, up, done
):
    (fetch,) = started([(up_hbm, up, done.at[1])])
    lat, half_index, near_index = place[0], place[3], place[4]
    for j in range(4):
        for half in range(2):
            column = pl.multiple_of(((half_index ^ half) * 4 + j) * 128, 128)
            for block in range(4):
                merged[ROWS * block : ROWS * block + ROWS, pl.ds(column, 128)] = columns[
                    j, block, :, 128 * half : 128 * half + 128
                ].astype(F32)
    own[...] = merged[pl.ds(pl.multiple_of(near_index * ROWS, 8), ROWS), :].astype(BF16)
    (copy,) = started([(own, own_merged, done.at[0])])
    normed[...] = norm_rows(merged[...]).astype(BF16)
    fetch.wait()
    value, rate = gelu_parts(dot(normed[...], up[...]))
    slope[:, 0:512] = rate.astype(BF16)
    bundle[:, 0:512] = value.astype(BF16)
    preact = 0.0
    for side, source in enumerate((near, far)):
        at = pl.ds(pl.multiple_of((lat ^ side) * 512, 512), 512)
        preact = preact + dot(normed[:, at], up_half(source))
    value, rate = gelu_parts(preact)
    slope[:, 512:1024] = rate.astype(BF16)
    bundle[:, 512:1024] = value.astype(BF16)
    bundle[:, 1024:1536] = stacked_rows(cots, pl.ds(pl.multiple_of((1 - lat) * 512, 512), 512))
    copy.wait()


def feed_kernel(
    place, up_hbm, down_hbm, slope_hbm, bundle, cots, near, far, s0, s1, s2, s3,
    values, grads, parts, up, down, slope, done,
):
    copies = started([(slope_hbm, slope, done.at[0]), (down_hbm, down, done.at[1]), (up_hbm, up, done.at[2])])
    cots = stacked_rows(cots, slice(0, 1024))
    far_values, far_hidden, far_grads = [0.0, 0.0], [], []
    for side, source in enumerate((near, far)):
        at = pl.ds(pl.multiple_of(512 + (place[0] ^ side) * 256, 256), 256)
        units = bundle[:, at]
        grad = 0.0
        for half in range(2):
            part = down_half(source, half)
            far_values[half] = far_values[half] + dot(units, part)
            grad = grad + dot_nt(cots[:, 512 * half : 512 * half + 512], part)
        far_hidden.append(grad)
    copies[0].wait()
    for side, grad in enumerate(far_hidden):
        at = pl.ds(pl.multiple_of(512 + (place[0] ^ side) * 256, 256), 256)
        far_grads.append((grad * slope[:, at].astype(F32)).astype(BF16))
    copies[1].wait()
    own_grad = (dot_nt(cots, down[...]) * slope[:, 0:512].astype(F32)).astype(BF16)
    values[...] = dot(bundle[:, 0:512], down[...]) + jnp.concatenate(far_values, axis=1)
    copies[2].wait()
    grads[...] = dot_nt(own_grad, up[...])
    first = jnp.where(place[0] == 0, far_grads[0].astype(F32), far_grads[1].astype(F32)).astype(BF16)
    second = jnp.where(place[0] == 0, far_grads[1].astype(F32), far_grads[0].astype(F32)).astype(BF16)
    grad = jnp.concatenate([first, second], axis=1)
    for side, source in enumerate((near, far)):
        at = pl.ds(pl.multiple_of((place[0] ^ side) * 512, 512), 512)
        grads[:, at] = grads[:, at] + dot_nt(grad, up_half(source))
    copies = []
    for j, sent in reversed(list(enumerate((s0, s1, s2, s3)))):
        at = pl.ds(pl.multiple_of((place[4] ^ j) * ROWS, 8), ROWS)
        parts[j, 0] = values[at, :].astype(BF16)
        parts[j, 1] = grads[at, :].astype(BF16)
        copies += started([(parts.at[j], sent, done.at[3 + j])])
    for copy in copies:
        copy.wait()


def sum_of(parts):
    summed = parts[0].astype(F32)
    for index in range(1, parts.shape[0]):
        summed = summed + parts[index].astype(F32)
    return summed


def finish_kernel(
    merged_hbm, cot_hbm, p0, p1, p2, p3, coarse_out, grad_merged, merged, cot, parts, first, second, done
):
    copies = started(
        [(merged_hbm, merged, done.at[0]), (cot_hbm.at[0], cot, done.at[1])]
        + [(p, parts.at[j], done.at[2 + j]) for j, p in enumerate((p0, p1, p2, p3))]
    )
    for copy in copies:
        copy.wait()
    merged_f = merged[...].astype(F32)
    value, grad_normed = merged_f, 0.0
    for j in range(4):
        value = value + parts[j, 0].astype(F32)
        grad_normed = grad_normed + parts[j, 1].astype(F32)
    value = value.astype(BF16)
    centred = merged_f - jnp.mean(merged_f, axis=-1, keepdims=True)
    scale_inv = lax.rsqrt(jnp.mean(centred * centred, axis=-1, keepdims=True) + EPS)
    nhat = centred * scale_inv
    grad = cot[...].astype(F32) + scale_inv * (
        grad_normed
        - jnp.mean(grad_normed, axis=-1, keepdims=True)
        - nhat * jnp.mean(grad_normed * nhat, axis=-1, keepdims=True)
    )
    grad = grad.astype(BF16)
    for lat in range(6):
        for lon in range(3):
            rows = slice(6 * lat + 2 * lon, 6 * lat + 2 * lon + 2)
            first[lat, lon] = value[rows]
            second[lat, lon] = grad[rows]
    copies = started([(first, coarse_out, done.at[0]), (second, grad_merged, done.at[1])])
    for copy in copies:
        copy.wait()


def finish(*args):
    tokens = shaped((6, 3, 2, 1024))
    return call(
        finish_kernel, (tokens, tokens), *args, hbm=range(6), hbm_out=2, flops=10**11,
        scratch_shapes=[
            pltpu.VMEM((ROWS, 1024), BF16),
            pltpu.VMEM((ROWS, 1024), BF16),
            pltpu.VMEM((4, 2, ROWS, 1024), BF16),
            pltpu.VMEM(tokens.shape, BF16),
            pltpu.VMEM(tokens.shape, BF16),
            pltpu.SemaphoreType.DMA((6,)),
        ],
    )


def weight_kernel(place, cots, bundle, other, slope, result, slope_hbm, held, done):
    copies = started([(slope, slope_hbm, done.at[2])])
    at = pl.ds(pl.multiple_of(place[0] * 512, 512), 512)
    rows = jnp.concatenate([stacked_rows(cots, at), other[:, 1024:1536]], axis=0)
    hidden = jnp.concatenate([bundle[:, 0:1024], other[:, 0:1024]], axis=0)
    for z_hi in range(2):
        total = dot_tn(rows[:, 256 * z_hi : 256 * z_hi + 256], hidden).astype(BF16)
        held[z_hi] = total.reshape(16, 16, 1024)
        copies += started([(held.at[z_hi], result.at[:, 16 * z_hi : 16 * z_hi + 16, :], done.at[z_hi])])
    for copy in copies:
        copy.wait()


def plane_sum_kernel(place, parts, result, total):
    total[...] = sum_of(parts)
    for z_hi in range(2):
        for half in range(2):
            at = pl.ds(pl.multiple_of((place[3] ^ half) * 512, 512), 512)
            result[2 * z_hi + half] = total[16 * z_hi : 16 * z_hi + 16, at].astype(BF16)


def line_sum_kernel(parts, result):
    result[...] = sum_of(parts)


def on_device(fine_tokens, fine_qkv, fine_out, merge_weight, up_weight, down_weight, cotangent):
    place = jnp.stack([lax.axis_index(a) for a in ("lat", "y", "x", "z_half", "z_near")]).astype(jnp.int32)
    side0, side1, piece, cot = prepare(fine_tokens, cotangent, merge_weight, up_weight, down_weight)

    got0 = swapped(side0, 1)
    got1 = moved(side1, lambda s: (s + 1 if s % 2 else s - 1) % COUNT)
    piece = along_z(piece)

    cots = exchanged(cot, "z_near")
    tokens, own = call(
        project_kernel, (shaped((144, 512)), shaped((144, 1536))), side0, side1, fine_qkv, hbm=range(2),
        flops=2 * 10**8, after=(cots,),
        scratch_shapes=[
            pltpu.VMEM((72, 512), BF16),
            pltpu.VMEM((96, 512), BF16),
            pltpu.SemaphoreType.DMA((2,)),
        ],
    )
    merged_in = call(
        attend_kernel, shaped((ROWS, 2048)), place, tokens, own, got0, got1, fine_qkv, fine_out,
        jnp.asarray(merge_order()), scalars=1, hbm_out=1, flops=10**9,
        scratch_shapes=[pltpu.VMEM((ROWS, 2048), BF16), pltpu.SemaphoreType.DMA],
    )
    pieces = call(
        spread_kernel, shaped((16, 80, 512)), piece, hbm_out=1, after=(merged_in,),
        scratch_shapes=[pltpu.SemaphoreType.DMA((16,))],
    )
    near = exchanged(pieces, ("y", "x"))
    ins = [merged_in] + [swapped(merged_in, j) for j in (3, 2, 1)][::-1]
    near = call(copy_kernel, shaped((16, 80, 512)), near, after=(merged_in,))
    far = across(near)
    narrow = shaped((4 * ROWS, 128), F32)
    rows, own, part = call(
        merge_near_kernel, (shaped((4 * ROWS, 2048)), narrow, narrow),
        place, *ins, merge_weight, near, scalars=1, hbm=(1,), flops=10**11,
        scratch_shapes=[
            pltpu.VMEM((ROWS, 2048), BF16),
            pltpu.VMEM((1024, 128), BF16),
            pltpu.SemaphoreType.DMA,
        ],
    )
    columns = call(
        merge_kernel, shaped((4, 4, ROWS, 256)), place, rows, own, part, far, scalars=1, flops=10**8,
        scratch_shapes=[pltpu.VMEM((1024, 128), BF16)],
    )
    columns = exchanged(columns, "z_near")
    own_merged, slope, bundle = call(
        hidden_kernel,
        (shaped((ROWS, 1024)), shaped((4 * ROWS, 1024)), shaped((4 * ROWS, 1536))),
        place, up_weight, columns, cots, near, far, scalars=1, hbm=(1,), hbm_out=1, flops=10**9,
        scratch_shapes=[
            pltpu.VMEM((4 * ROWS, 1024), F32),
            pltpu.VMEM((ROWS, 1024), BF16),
            pltpu.VMEM((4 * ROWS, 1024), BF16),
            pltpu.VMEM((1024, 512), BF16),
            pltpu.SemaphoreType.DMA((2,)),
        ],
    )
    other = across(bundle)
    parts, slope = call(
        weight_kernel, (shaped((16, 32, 1024)), shaped((4 * ROWS, 1024))), place, cots, bundle, other, slope,
        scalars=1, hbm_out=2, flops=3 * 10**8,
        scratch_shapes=[pltpu.VMEM((2, 16, 16, 1024), BF16), pltpu.SemaphoreType.DMA((3,))],
    )
    parts = exchanged(parts, ("y", "x"))
    partial = shaped((2, ROWS, 1024))
    partials = call(
        feed_kernel, (partial,) * 4, place, up_weight, down_weight, slope, bundle, cots, near, far, scalars=1,
        hbm=range(1, 4), hbm_out=4, flops=2 * 10**9,
        scratch_shapes=[
            pltpu.VMEM((4 * ROWS, 1024), F32),
            pltpu.VMEM((4 * ROWS, 1024), F32),
            pltpu.VMEM((4, 2, ROWS, 1024), BF16),
            pltpu.VMEM((1024, 512), BF16),
            pltpu.VMEM((512, 1024), BF16),
            pltpu.VMEM((4 * ROWS, 1024), BF16),
            pltpu.SemaphoreType.DMA((7,)),
        ],
    )
    partials = [partials[0]] + [swapped(partials[j], j) for j in (3, 2, 1)][::-1]
    parts = call(
        plane_sum_kernel, shaped((4, 16, 512)), place, parts, scalars=1,
        scratch_shapes=[pltpu.VMEM((32, 1024), F32)],
    )
    parts = exchanged(parts, ("z_hi", "z_half"))
    coarse_out, grad_merged = finish(own_merged, cot, *partials)
    grad_down, coarse_out, grad_merged = call(
        line_sum_kernel, shaped((16, 512), F32), parts, through=(coarse_out, grad_merged)
    )
    grad_down = grad_down.T
    return coarse_out.transpose(2, 0, 1, 3), grad_merged.transpose(2, 0, 1, 3), grad_down


def solution(mesh):
    lon, tp = ("z_hi", "y", "x"), ("z_half", "z_near")
    parts = Mesh(mesh.devices.reshape(2, 2, 4, 4, 2, 4), AXES)
    tokens = P(None, "lat", lon + tp, None)
    return jax.shard_map(
        on_device,
        mesh=parts,
        in_specs=(tokens, P(), P(), P(None, tp), P(None, tp), P(tp, None), tokens),
        out_specs=(tokens, tokens, P(tp, ("lat",) + lon)),
        check_vma=False,
    )
```
